768 devices in a mesh: segment: 4 (over y_hi, core), lane: 4 (over x), dp: 48 (over y_lo, z).
Axes of the slice: x: 4, y: 8 (y_hi: 2, y_lo: 4; y = y_hi * 4 + y_lo), z: 12, core: 2. Of those that a mesh axis runs over, the one named last changes fastest.
Arguments:
- inputs: bfloat16 [4, 2, 3072, 3072], P('segment', None, 'dp', 'lane'), may hold values from -6 to 6
- gate_sums: bfloat16 [4, 2, 3072, 3264], P('segment', None, 'dp', 'lane'), may hold values from -6 to 6
- top_grads: bfloat16 [2, 3072, 3072], P(None, 'dp', 'lane'), may hold values from -6 to 6
- up_weight: bfloat16 [4, 3072, 3264], P('segment', None, 'lane'), may hold values from -0.109375 to 0.109375
- down_weight: bfloat16 [4, 3264, 3072], P('segment', 'lane'), may hold values from -0.109375 to 0.109375
- projectors: bfloat16 [4, 2, 3264, 128], P('segment', None, 'lane'), may hold values from -1 to 1, as said below
- first_moment: float32 [4, 4, 2, 128, 3072], P('segment', 'lane', None, None, 'dp'), may hold values from -48 to 48
- second_moment: float32 [4, 4, 2, 128, 3072], P('segment', 'lane', None, None, 'dp'), may hold values from 122.88 to 3072
Outputs:
- input_grads: bfloat16 [4, 2, 3072, 3072], P('segment', None, 'dp', 'lane')
- new_first: float32 [4, 4, 2, 128, 3072], P('segment', 'lane', None, None, 'dp')
- new_second: float32 [4, 4, 2, 128, 3072], P('segment', 'lane', None, None, 'dp')
- new_up: bfloat16 [4, 3072, 3264], P('segment', 'dp', 'lane')
- new_down: bfloat16 [4, 3264, 3072], P('segment', 'lane', 'dp')
The draws below stay inside these ranges and needn't reach their ends.
Inputs may be any that keep to these rules, and one draw needn't show every extreme that they name: For every section, kind and lane, the 816 rows of projectors that belong to that lane form a matrix with orthonormal columns, up to bfloat16 rounding.
All inputs are finite; a program needn't handle non-finite values.
Results may differ from the reference program's by a relative error of at most 0.018.
Values may be sent and summed in bfloat16 or wider, within the bound.
A program may use at most 64 MiB of HBM per device.

```python
import math
import jax
import jax.numpy as jnp
from jax import lax

D = 3072
FF_DEV = 816
RANK = 128
M = 2
SEGMENTS = 4
LANES = 4
TOKENS = 3072
FF = 3264


def draw_projectors(key, part):
    gaussian = jax.random.normal(jax.random.fold_in(key, 7), (SEGMENTS, 2, LANES, FF_DEV, RANK), jnp.float32)
    ortho_basis, upper_part = jnp.linalg.qr(gaussian)
    return ortho_basis.reshape(SEGMENTS, 2, LANES * FF_DEV, RANK).astype(jnp.bfloat16)


def with_spikes(array, key, source, target, shards_of, factor):
    def block_of(position):
        return (jnp.arange(array.shape[position]) // (array.shape[position] // shards_of)).reshape((-1,) + (1,) * (array.ndim - 1 - position))

    one_side = jax.random.permutation(key, shards_of)[block_of(target)]
    far = (block_of(target) + shards_of // 2) % shards_of
    return jnp.where((block_of(source) == one_side) | (block_of(source) == far), factor * array, array)


def levels(key, extent, shards, low, high):
    level, own = 1.0, jax.random.fold_in(key, 6)
    for axis_at, blocks in shards:
        draws = jnp.exp(jax.random.uniform(jax.random.fold_in(own, axis_at), (blocks,), jnp.float32, low / len(shards), high / len(shards)))
        level = level * jnp.repeat(draws, extent[axis_at] // blocks).reshape([-1 if axis == axis_at else 1 for axis in range(len(extent))])
    return level


def scatter_about(stream_key, dims, spread, most, pieces=(), kind=jnp.bfloat16):
    entries = spread * jax.random.normal(stream_key, dims, jnp.float32)
    if pieces:
        entries = entries * levels(stream_key, dims, pieces, -0.22, 0.18)
    return jnp.clip(entries, -most, most).astype(kind)


def noise_with(own_key, shape, deviation, limit, pieces, heavy, kind=jnp.bfloat16):
    values = deviation * jax.random.normal(own_key, shape, jnp.float32)
    if pieces:
        values = values * levels(own_key, shape, pieces, -0.22, 0.18)
    return jnp.clip(with_spikes(values, jax.random.fold_in(own_key, 3), *heavy), -limit, limit).astype(kind)


def setup_inputs(seed: int = 0) -> dict:
    streams_of = jax.random.split(jax.random.key(seed), 9)
    return {
        "inputs": noise_with(streams_of[0], (SEGMENTS, M, TOKENS, D), 1.0, 6.0, ((0, 4), (2, 48), (3, 4)), (2, 3, 48, 3.25)),
        "gate_sums": scatter_about(streams_of[1], (SEGMENTS, M, TOKENS, FF), 1.0, 6.0, ((0, 4), (2, 48), (3, 4))),
        "top_grads": scatter_about(streams_of[2], (M, TOKENS, D), 1.0, 6.0, ((1, 48), (2, 4))),
        "up_weight": scatter_about(streams_of[3], (SEGMENTS, D, FF), D ** -0.5, 0.109375, ((0, 4), (2, 4))),
        "down_weight": scatter_about(streams_of[4], (SEGMENTS, FF, D), FF ** -0.5, 0.109375, ((0, 4), (1, 4))),
        "projectors": draw_projectors(jax.random.fold_in(streams_of[8], 71), 0),
        "first_moment": scatter_about(streams_of[6], (SEGMENTS, LANES, 2, RANK, D), (0.1 * (M * TOKENS) ** 0.5), 48.0, ((0, 4), (1, 4), (4, 48)), jnp.float32),
        "second_moment": jnp.clip(jnp.exp(math.log(3072.0) - 3.218876 * jax.random.uniform(streams_of[7], (SEGMENTS, LANES, 2, RANK, D), jnp.float32) ** levels(streams_of[7], (SEGMENTS, LANES, 2, RANK, D), ((0, 4), (1, 4), (4, 48)), -0.2, 0.2)), 122.88, 3072.0),
    }


def reference(inputs, gate_sums, top_grads, up_weight, down_weight, projectors, first_moment, second_moment):
    grads_by_segment = [None] * SEGMENTS
    first_by_segment = [None] * SEGMENTS
    second_by_segment = [None] * SEGMENTS
    up_by_segment = [None] * SEGMENTS
    down_by_segment = [None] * SEGMENTS
    cotangents = top_grads
    contract_cols = (((1,), (1,)), ((), ()))
    contract_rows = (((0,), (0,)), ((), ()))
    for segment_index in reversed(range(SEGMENTS)):
        weight_up = up_weight[segment_index]
        weight_down = down_weight[segment_index]
        proj_up = projectors[segment_index, 0]
        proj_down = projectors[segment_index, 1]
        code_total = jnp.zeros((LANES, 2, RANK, D), jnp.float32)
        segment_grads = []
        for micro_index in range(M):
            cotangent = cotangents[micro_index]
            input_rows = inputs[segment_index, micro_index]
            up_value = jnp.dot(input_rows.astype(jnp.float32), weight_up.astype(jnp.float32), preferred_element_type=jnp.float32)
            gate_act = jax.nn.silu(gate_sums[segment_index, micro_index].astype(jnp.float32))
            hidden = (gate_act * up_value).astype(jnp.bfloat16)
            hidden_grad = lax.dot_general(cotangent.astype(jnp.float32), weight_down.astype(jnp.float32), contract_cols, preferred_element_type=jnp.float32)
            up_grad = (hidden_grad * gate_act).astype(jnp.bfloat16)
            summed = cotangent.astype(jnp.float32)
            for lane_index in range(LANES):
                low = lane_index * FF_DEV
                high = low + FF_DEV
                part = lax.dot_general(up_grad[:, low:high].astype(jnp.float32), weight_up[:, low:high].astype(jnp.float32), contract_cols, preferred_element_type=jnp.float32)
                part = lax.optimization_barrier(part.astype(jnp.bfloat16))
                summed = summed + part.astype(jnp.float32)
                code_up = jnp.dot(up_grad[:, low:high].astype(jnp.float32), proj_up[low:high].astype(jnp.float32), preferred_element_type=jnp.float32).astype(jnp.bfloat16)
                code_down = jnp.dot(hidden[:, low:high].astype(jnp.float32), proj_down[low:high].astype(jnp.float32), preferred_element_type=jnp.float32).astype(jnp.bfloat16)
                term_up = lax.dot_general(code_up.astype(jnp.float32), input_rows.astype(jnp.float32), contract_rows, preferred_element_type=jnp.float32)
                term_down = lax.dot_general(code_down.astype(jnp.float32), cotangent.astype(jnp.float32), contract_rows, preferred_element_type=jnp.float32)
                code_total = code_total.at[lane_index].add(jnp.stack([term_up, term_down]))
            segment_grads.append(summed.astype(jnp.bfloat16))
        segment_grads = jnp.stack(segment_grads)
        grads_by_segment[segment_index] = segment_grads
        cotangents = segment_grads
        first_next = 0.9 * first_moment[segment_index] + 0.1 * code_total
        second_next = 0.999 * second_moment[segment_index] + 0.001 * code_total * code_total
        step_code = first_next / (jnp.sqrt(second_next) + 1e-08)
        first_by_segment[segment_index] = first_next
        second_by_segment[segment_index] = second_next
        up_blocks = []
        down_blocks = []
        for lane_index in range(LANES):
            low = lane_index * FF_DEV
            high = low + FF_DEV
            delta_up = lax.dot_general(step_code[lane_index, 0], proj_up[low:high].astype(jnp.float32), (((0,), (1,)), ((), ())), precision=lax.Precision.HIGHEST)
            up_blocks.append((weight_up[:, low:high].astype(jnp.float32) - 0.05 * delta_up).astype(jnp.bfloat16))
            delta_down = jnp.dot(proj_down[low:high].astype(jnp.float32), step_code[lane_index, 1], precision=lax.Precision.HIGHEST)
            down_blocks.append((weight_down[low:high].astype(jnp.float32) - 0.05 * delta_down).astype(jnp.bfloat16))
        up_by_segment[segment_index] = jnp.concatenate(up_blocks, axis=1)
        down_by_segment[segment_index] = jnp.concatenate(down_blocks, axis=0)
    return (jnp.stack(grads_by_segment), jnp.stack(first_by_segment), jnp.stack(second_by_segment), jnp.stack(up_by_segment), jnp.stack(down_by_segment))
```

```python
import functools

import jax
import jax.numpy as jnp
from jax import lax
from jax.experimental import pallas as pl
from jax.experimental.pallas import tpu as pltpu
from jax.sharding import PartitionSpec as P

MESH = pl.DeviceIdType.MESH
NT = (((1,), (1,)), ((), ()))
NN = (((1,), (0,)), ((), ()))
TN = (((0,), (0,)), ((), ()))
BF = jnp.bfloat16
F32 = jnp.float32


def mm(a, b, dims):
    return lax.dot_general(a, b, dims, preferred_element_type=F32)


def kernel(
    zn,
    x_hbm, gate_hbm, top_hbm, wu_hbm, wd_hbm, proj_hbm, m1_hbm, m2_hbm,
    og_hbm, nf_hbm, ns_hbm, nu_hbm, nd_hbm,
    wu, wd, proj, gate, m1, m2,
    xg, cg, act, acc, ug, hid, part, prs, og,
    cup, cdn, terms, zsrc, zrecv, ysend, yrecv, ykeep,
    base, nfv, nsv, nwv,
    loc, wsem, out_sem,
    ag_s, bc_s, ag_r, yh_s, yh_r, in_s, in_r, rs_s, rs_r, z_s, z_r, y_s, y_r,
):
    s = lax.axis_index("segment")
    l = lax.axis_index("lane")
    dp = lax.axis_index("dp")
    z = lax.rem(dp, zn)
    y = dp // zn
    odd = lax.rem(s, 2) == 1
    pair = s + 1 - 2 * lax.rem(s, 2)

    def lane(k):
        return lax.rem(l + k, 4)

    def zdev(k):
        return y * zn + lax.rem(z + k + zn, zn)

    def ydev(k):
        return lax.rem(y + k, 4) * zn + z

    loads = [
        pltpu.make_async_copy(gate_hbm, gate, loc.at[0]),
        pltpu.make_async_copy(x_hbm, xg.at[l], loc.at[1]),
        pltpu.make_async_copy(proj_hbm, proj, loc.at[2]),
        pltpu.make_async_copy(m1_hbm, m1, loc.at[3]),
        pltpu.make_async_copy(m2_hbm, m2, loc.at[4]),
    ]
    wd_loads = [
        pltpu.make_async_copy(wd_hbm.at[:, pl.ds(kb * 768, 768)], wd.at[kb], wsem.at[0, kb])
        for kb in range(4)
    ]
    wu_loads = [
        pltpu.make_async_copy(wu_hbm.at[:, pl.ds(kb * 768, 768)], wu.at[kb], wsem.at[1, kb])
        for kb in range(4)
    ]
    top_load = pltpu.make_async_copy(top_hbm, cg.at[l], loc.at[5])

    @pl.when(s == 3)
    def _():
        top_load.start()

    for c in wd_loads + wu_loads + loads:
        c.start()

    barrier = pltpu.get_barrier_semaphore()

    def greet(dev):
        pl.semaphore_signal(barrier, inc=1, device_id=dev, device_id_type=MESH)

    for k in (1, 2, 3):
        greet({"lane": lane(k)})
        greet({"dp": ydev(k)})
    for k in range(4):
        greet({"segment": pair, "lane": lane(k)})
    greet({"segment": 3 - s})
    greet({"dp": zdev(1)})
    greet({"dp": zdev(-1)})
    pl.semaphore_wait(barrier, 13)

    def remote(src, dst, ss, rr, dev):
        return pltpu.make_async_remote_copy(
            src_ref=src, dst_ref=dst, send_sem=ss, recv_sem=rr, device_id=dev, device_id_type=MESH
        )

    def gather_top(u, k):
        return remote(top_hbm.at[u], cg.at[l, u], ag_s.at[u, k], ag_r.at[u, k], {"lane": lane(k)})

    def gather_cot(u, k):
        return remote(cg.at[l, u], cg.at[l, u], ag_s.at[u, k], ag_r.at[u, k], {"lane": lane(k)})

    def gather_in(k):
        return remote(x_hbm, xg.at[l], in_s.at[k], in_r.at[k], {"lane": lane(k)})

    def cast_down(u, k):
        return remote(
            og.at[u], cg.at[l, u], bc_s.at[u, k], ag_r.at[u, k], {"segment": pair, "lane": lane(k)}
        )

    def hop(u):
        return remote(og.at[u], cg.at[l, u], yh_s.at[u], yh_r.at[u], {"segment": 3 - s})

    def scatter(u, k):
        return remote(part.at[u, k], prs.at[u, k], rs_s.at[u, k], rs_r.at[u, k], {"lane": lane(k)})

    ORDER = (2, 1, 3)

    @pl.when(s == 3)
    def _():
        for u in range(2):
            for k in ORDER:
                gather_top(u, k).start()

    for c in loads:
        c.wait()
    v = gate[...].reshape(128, 816).astype(F32)
    act[...] = v / (1.0 + jnp.exp(-v))

    for c in wd_loads:
        c.wait()
    for c in wu_loads:
        c.wait()

    for k in ORDER:
        gather_in(k).start()

    @pl.when(s == 3)
    def _():
        top_load.wait()

    pick = lax.broadcasted_iota(jnp.int32, (64, 128), 0) + 64 * lax.rem(z, 2)
    pick = (lax.broadcasted_iota(jnp.int32, (64, 128), 1) == pick).astype(BF)
    at = pl.ds(pl.multiple_of((z // 2) * 128, 128), 128)
    base[0] = mm(pick, wu[y, :, at], NT)
    base[1] = mm(pick, wd[y, :, at], NT)

    def prep():
        for k in (0, 1, 3, 2):
            kb = lane(4 - k)
            if k:
                gather_in(k).wait_recv()
            r = mm(xg[kb].reshape(128, 768), wu[kb], NT)
            if k == 0:
                acc[...] = r
            else:
                acc[...] += r
        hid[...] = (acc[...] * act[...]).astype(BF)
        cdn[...] = mm(hid[...], proj[1], NN).astype(BF)

    @pl.when(s < 3)
    def _():
        prep()

    def first(u):
        rows = slice(u * 64, u * 64 + 64)

        @pl.when(s == 1)
        def _():
            hop(u).wait_recv()
            for k in ORDER:
                gather_cot(u, k).start()

        for k in (0, 1, 3, 2):
            kb = lane(4 - k)
            if k:
                gather_cot(u, k).wait_recv()
            else:
                @pl.when(jnp.logical_not(odd))
                def _():
                    cast_down(u, 0).wait_recv()
            r = mm(cg[kb, u], wd[kb], NT)
            if k == 0:
                acc[0:64, :] = r
            else:
                acc[0:64, :] += r
        ug[rows, :] = (acc[0:64, :] * act[rows, :]).astype(BF)

    def second(u):
        rows = slice(u * 64, u * 64 + 64)
        for k in (2, 1, 3, 0):
            part[u, k] = mm(ug[rows, :], wu[lane(k)], NN).astype(BF)
            if k:
                scatter(u, k).start()

    def finish(u):
        total = cg[l, u].astype(F32) + part[u, 0].astype(F32)
        for k in (1, 3, 2):
            scatter(u, k).wait_recv()
            total += prs[u, k].astype(F32)
        og[u] = total.astype(BF)

        @pl.when(odd)
        def _():
            for k in (2, 1, 3, 0):
                cast_down(u, k).start()

        @pl.when(s == 2)
        def _():
            hop(u).start()

        pltpu.make_async_copy(og.at[u], og_hbm.at[u], out_sem.at[u]).start()

    def zcount(t, d):
        return 6 if t == d else 5

    def owner(n, d, k):
        return lax.rem(z + (n - k if d else k - n) + zn, zn)

    def zcopy(t, d, k):
        src = zsrc.at[t, d] if k == 0 else zrecv.at[t, d, k - 1]
        return remote(
            src, zrecv.at[t, d, k], z_s.at[t, d, k], z_r.at[t, d, k], {"dp": zdev(1 if d else -1)}
        )

    def ring_start(t):
        for d in range(2):
            zsrc[t, d] = terms[t, :, owner(zcount(t, d), d, 0)].astype(BF)
            zcopy(t, d, 0).start()

    def ring_step(t, k):
        for d in range(2):
            n = zcount(t, d)
            if k < n:
                zcopy(t, d, k - 1).wait_recv()
                mine = terms[t, :, owner(n, d, k)]
                zrecv[t, d, k - 1] = (zrecv[t, d, k - 1].astype(F32) + mine).astype(BF)
                zcopy(t, d, k).start()

    def make_term(t):
        rows_of, code = (xg, cup) if t == 0 else (cg, cdn)
        for kb in range(4):
            r = mm(rows_of[kb].reshape(128, 768), code[...], TN)
            terms[t, kb] = r.reshape(zn, 64, 128)

    def codes():
        cup[...] = mm(ug[...], proj[0], NN).astype(BF)
        for t in range(2):
            make_term(t)
            ring_start(t)

    first(0)
    second(0)
    first(1)

    @pl.when(s == 0)
    def _():
        finish(0)
        codes()

    second(1)

    @pl.when(s > 0)
    def _():
        finish(0)
        finish(1)

        @pl.when(s == 3)
        def _():
            prep()

        codes()

    for k in range(1, 6):
        for t in range(2):
            ring_step(t, k)
        if k == 3:
            @pl.when(s == 0)
            def _():
                finish(1)

    def ycopy(t, k):
        return remote(
            ysend.at[t, k], yrecv.at[t, k], y_s.at[t, k], y_r.at[t, k], {"dp": ydev(k)}
        )

    for t in range(2):
        for d in range(2):
            zcopy(t, d, zcount(t, d) - 1).wait_recv()
        for k in (3, 2, 1, 0):
            yo = lax.rem(y + k, 4)
            r = terms[t, yo, z]
            for d in range(2):
                r += zrecv[t, d, zcount(t, d) - 1, yo].astype(F32)
            if k:
                ysend[t, k] = r.astype(BF)
                ycopy(t, k).start()
            else:
                ykeep[t] = r

    outs = []
    for t in range(2):
        grad = ykeep[t]
        for k in (1, 2, 3):
            ycopy(t, k).wait_recv()
            grad += yrecv[t, k].astype(F32)
        new_first = 0.9 * m1[t] + 0.1 * grad
        new_second = 0.999 * m2[t] + 0.001 * grad * grad
        nfv[t] = new_first
        nsv[t] = new_second
        step = new_first / (jnp.sqrt(new_second) + 1e-08)
        high = step.astype(BF)
        low = (step - high.astype(F32)).astype(BF)
        delta = mm(high, proj[t], NT) + mm(low, proj[t], NT)
        nwv[t] = (base[t] - 0.05 * delta).astype(BF)
        outs += [
            pltpu.make_async_copy(nfv.at[t], nf_hbm.at[t], out_sem.at[2 + 3 * t]),
            pltpu.make_async_copy(nsv.at[t], ns_hbm.at[t], out_sem.at[3 + 3 * t]),
            pltpu.make_async_copy(nwv.at[t], (nu_hbm, nd_hbm)[t], out_sem.at[4 + 3 * t]),
        ]
        for c in outs[-3:]:
            c.start()

    @pl.when(s == 3)
    def _():
        for u in range(2):
            for k in ORDER:
                gather_top(u, k).wait_send()

    @pl.when(s == 1)
    def _():
        for u in range(2):
            for k in ORDER:
                gather_cot(u, k).wait_send()

    @pl.when(odd)
    def _():
        for u in range(2):
            for k in range(4):
                cast_down(u, k).wait_send()

    @pl.when(s == 2)
    def _():
        for u in range(2):
            hop(u).wait_send()

    for k in ORDER:
        gather_in(k).wait_send()
        for u in range(2):
            scatter(u, k).wait_send()
            ycopy(u, k).wait_send()
    for t in range(2):
        for d in range(2):
            for k in range(zcount(t, d)):
                zcopy(t, d, k).wait_send()
    for u in range(2):
        pltpu.make_async_copy(og.at[u], og_hbm.at[u], out_sem.at[u]).wait()
    for c in outs:
        c.wait()


def local(zn, inputs, gate_sums, top_grads, up_weight, down_weight, projectors, first_moment, second_moment):
    sds = jax.ShapeDtypeStruct
    any_spec = pl.BlockSpec(memory_space=pl.ANY)
    dma = pltpu.SemaphoreType.DMA
    og, nf, ns, nu, nd = pl.pallas_call(
        functools.partial(kernel, zn),
        out_shape=(
            sds((2, 64, 768), BF),
            sds((2, 64, 128), F32),
            sds((2, 64, 128), F32),
            sds((64, 816), BF),
            sds((64, 816), BF),
        ),
        in_specs=[any_spec] * 8,
        out_specs=(any_spec,) * 5,
        scratch_shapes=[
            pltpu.VMEM((4, 816, 768), BF),
            pltpu.VMEM((4, 816, 768), BF),
            pltpu.VMEM((2, 816, 128), BF),
            pltpu.VMEM((2, 64, 816), BF),
            pltpu.VMEM((2, 64, 128), F32),
            pltpu.VMEM((2, 64, 128), F32),
            pltpu.VMEM((4, 2, 64, 768), BF),
            pltpu.VMEM((4, 2, 64, 768), BF),
            pltpu.VMEM((128, 816), F32),
            pltpu.VMEM((128, 816), F32),
            pltpu.VMEM((128, 816), BF),
            pltpu.VMEM((128, 816), BF),
            pltpu.VMEM((2, 4, 64, 768), BF),
            pltpu.VMEM((2, 4, 64, 768), BF),
            pltpu.VMEM((2, 64, 768), BF),
            pltpu.VMEM((128, 128), BF),
            pltpu.VMEM((128, 128), BF),
            pltpu.VMEM((2, 4, zn, 64, 128), F32),
            pltpu.VMEM((2, 2, 4, 64, 128), BF),
            pltpu.VMEM((2, 2, 6, 4, 64, 128), BF),
            pltpu.VMEM((2, 4, 64, 128), BF),
            pltpu.VMEM((2, 4, 64, 128), BF),
            pltpu.VMEM((2, 64, 128), F32),
            pltpu.VMEM((2, 64, 816), F32),
            pltpu.VMEM((2, 64, 128), F32),
            pltpu.VMEM((2, 64, 128), F32),
            pltpu.VMEM((2, 64, 816), BF),
            dma((6,)),
            dma((2, 4)),
            dma((8,)),
            dma((2, 4)),
            dma((2, 4)),
            dma((2, 4)),
            dma((2,)),
            dma((2,)),
            dma((4,)),
            dma((4,)),
            dma((2, 4)),
            dma((2, 4)),
            dma((2, 2, 6)),
            dma((2, 2, 6)),
            dma((2, 4)),
            dma((2, 4)),
        ],
        compiler_params=pltpu.CompilerParams(
            collective_id=0, has_side_effects=True, vmem_limit_bytes=60 * 2**20
        ),
        name="relay",
    )(
        inputs[0],
        gate_sums[0],
        top_grads,
        jnp.swapaxes(up_weight[0], 0, 1),
        down_weight[0],
        projectors[0],
        jnp.swapaxes(first_moment[0, 0], 1, 2),
        jnp.swapaxes(second_moment[0, 0], 1, 2),
    )
    return (
        og[None],
        jnp.swapaxes(nf, 1, 2)[None, None],
        jnp.swapaxes(ns, 1, 2)[None, None],
        nu[None],
        jnp.swapaxes(nd, 0, 1)[None],
    )


def solution(mesh):
    placed = (
        P("segment", None, "dp", "lane"),
        P("segment", None, "dp", "lane"),
        P(None, "dp", "lane"),
        P("segment", None, "lane"),
        P("segment", "lane", None),
        P("segment", None, "lane", None),
        P("segment", "lane", None, None, "dp"),
        P("segment", "lane", None, None, "dp"),
    )
    return jax.shard_map(
        functools.partial(local, mesh.shape["dp"] // 4),
        mesh=mesh,
        in_specs=placed,
        out_specs=(
            P("segment", None, "dp", "lane"),
            P("segment", "lane", None, None, "dp"),
            P("segment", "lane", None, None, "dp"),
            P("segment", "dp", "lane"),
            P("segment", "lane", "dp"),
        ),
        check_vma=False,
    )
```

```python
import contextlib
import functools

import jax
import jax.numpy as jnp
from jax import lax
from jax.experimental import pallas as pl
from jax.experimental.pallas import tpu as pltpu
from jax.sharding import PartitionSpec as P

MESH = pl.DeviceIdType.MESH
scope = contextlib.nullcontext
NT = (((1,), (1,)), ((), ()))
NN = (((1,), (0,)), ((), ()))
TN = (((0,), (0,)), ((), ()))
BF = jnp.bfloat16
F32 = jnp.float32


def mm(a, b, dims):
    return lax.dot_general(a, b, dims, preferred_element_type=F32)


def kernel(
    zn,
    x_hbm, gate_hbm, top_hbm, wu_hbm, wd_hbm, proj_hbm, m1_hbm, m2_hbm,
    og, nfv, nsv, nup, ndown,
    wu, wd, proj, gate, m1, m2,
    xg, cg, act, acc, ug, hid, part, prs,
    cup, cdn, terms, zsrc, zrecv, ysend, yrecv, ykeep,
    base,
    loc, wsem,
    ag_s, bc_s, ag_r, yh_s, yh_r, in_s, in_r, rs_s, rs_r, z_s, z_r, y_s, y_r,
):
    s = lax.axis_index("segment")
    l = lax.axis_index("lane")
    dp = lax.axis_index("dp")
    z = lax.rem(dp, zn)
    y = dp // zn
    odd = lax.rem(s, 2) == 1
    pair = s + 1 - 2 * lax.rem(s, 2)

    def lane(k):
        return lax.rem(l + k, 4)

    def zdev(k):
        return y * zn + lax.rem(z + k + zn, zn)

    def ydev(k):
        return lax.rem(y + k, 4) * zn + z

    loads = [
        pltpu.make_async_copy(gate_hbm, gate, loc.at[0]),
        pltpu.make_async_copy(x_hbm, xg.at[l], loc.at[1]),
        pltpu.make_async_copy(proj_hbm, proj, loc.at[2]),
        pltpu.make_async_copy(m1_hbm, m1, loc.at[3]),
        pltpu.make_async_copy(m2_hbm, m2, loc.at[4]),
    ]
    wd_loads = [
        pltpu.make_async_copy(wd_hbm.at[:, pl.ds(kb * 768, 768)], wd.at[kb], wsem.at[0, kb])
        for kb in range(4)
    ]
    wu_loads = [
        pltpu.make_async_copy(wu_hbm.at[:, pl.ds(kb * 768, 768)], wu.at[kb], wsem.at[1, kb])
        for kb in range(4)
    ]
    top_load = pltpu.make_async_copy(top_hbm, cg.at[l], loc.at[5])

    @pl.when(s == 3)
    def _():
        top_load.start()

    for c in wd_loads + wu_loads + loads:
        c.start()

    barrier = pltpu.get_barrier_semaphore()

    def greet(dev):
        pl.semaphore_signal(barrier, inc=1, device_id=dev, device_id_type=MESH)

    for k in (1, 2, 3):
        greet({"lane": lane(k)})
        greet({"dp": ydev(k)})
    for k in range(4):
        greet({"segment": pair, "lane": lane(k)})
    greet({"segment": 3 - s})
    greet({"dp": zdev(1)})
    greet({"dp": zdev(-1)})
    with scope("entry"):
        pl.semaphore_wait(barrier, 13)

    def remote(src, dst, ss, rr, dev):
        return pltpu.make_async_remote_copy(
            src_ref=src, dst_ref=dst, send_sem=ss, recv_sem=rr, device_id=dev, device_id_type=MESH
        )

    def gather_top(u, k):
        return remote(top_hbm.at[u], cg.at[l, u], ag_s.at[u, k], ag_r.at[u, k], {"lane": lane(k)})

    def gather_cot(u, k):
        return remote(cg.at[l, u], cg.at[l, u], ag_s.at[u, k], ag_r.at[u, k], {"lane": lane(k)})

    def gather_in(k):
        return remote(x_hbm, xg.at[l], in_s.at[k], in_r.at[k], {"lane": lane(k)})

    def cast_down(u, k):
        return remote(
            og.at[u], cg.at[l, u], bc_s.at[u, k], ag_r.at[u, k], {"segment": pair, "lane": lane(k)}
        )

    def hop(u):
        return remote(og.at[u], cg.at[l, u], yh_s.at[u], yh_r.at[u], {"segment": 3 - s})

    def scatter(u, k):
        return remote(part.at[u, k], prs.at[u, k], rs_s.at[u, k], rs_r.at[u, k], {"lane": lane(k)})

    ORDER = (2, 1, 3)

    @pl.when(s == 3)
    def _():
        for u in range(2):
            for k in ORDER:
                gather_top(u, k).start()

    with scope("act"):
        for c in loads:
            c.wait()
        v = gate[...].reshape(128, 816).astype(F32)
        act[...] = v / (1.0 + jnp.exp(-v))

    with scope("weights"):
        for c in wd_loads:
            c.wait()
        for c in wu_loads:
            c.wait()

    for k in ORDER:
        gather_in(k).start()

    @pl.when(s == 3)
    def _():
        top_load.wait()

    pick = lax.broadcasted_iota(jnp.int32, (64, 128), 0) + 64 * lax.rem(z, 2)
    pick = (lax.broadcasted_iota(jnp.int32, (64, 128), 1) == pick).astype(BF)
    at = pl.ds(pl.multiple_of((z // 2) * 128, 128), 128)
    base[0] = mm(pick, wu[y, :, at], NT)
    base[1] = mm(pick, wd[y, :, at], NT)

    def prep():
        for k in (0, 1, 3, 2):
            kb = lane(4 - k)
            with scope("prepwait"):
                if k:
                    gather_in(k).wait_recv()
            r = mm(xg[kb].reshape(128, 768), wu[kb], NT)
            if k == 0:
                acc[...] = r
            else:
                acc[...] += r
        hid[...] = (acc[...] * act[...]).astype(BF)
        cdn[...] = mm(hid[...], proj[1], NN).astype(BF)

    @pl.when(s < 3)
    def _():
        prep()

    def first(u):
        rows = slice(u * 64, u * 64 + 64)

        @pl.when(s == 1)
        def _():
            with scope("hopwait"):
                hop(u).wait_recv()
            for k in ORDER:
                gather_cot(u, k).start()

        for k in (0, 1, 3, 2):
            kb = lane(4 - k)
            with scope("cotwait"):
                if k:
                    gather_cot(u, k).wait_recv()
                else:
                    @pl.when(jnp.logical_not(odd))
                    def _():
                        cast_down(u, 0).wait_recv()
            r = mm(cg[kb, u], wd[kb], NT)
            if k == 0:
                acc[0:64, :] = r
            else:
                acc[0:64, :] += r
        ug[rows, :] = (acc[0:64, :] * act[rows, :]).astype(BF)

    def second(u):
        rows = slice(u * 64, u * 64 + 64)
        for k in (2, 1, 3, 0):
            part[u, k] = mm(ug[rows, :], wu[lane(k)], NN).astype(BF)
            if k:
                scatter(u, k).start()

    def finish(u):
        total = cg[l, u].astype(F32) + part[u, 0].astype(F32)
        for k in (1, 3, 2):
            with scope("scatwait"):
                scatter(u, k).wait_recv()
            total += prs[u, k].astype(F32)
        og[u] = total.astype(BF)

        @pl.when(odd)
        def _():
            for k in (2, 1, 3, 0):
                cast_down(u, k).start()

        @pl.when(s == 2)
        def _():
            hop(u).start()

    def zcount(t, d):
        return 6 if t == d else 5

    def owner(n, d, k):
        return lax.rem(z + (n - k if d else k - n) + zn, zn)

    def zcopy(t, d, k):
        src = zsrc.at[t, d] if k == 0 else zrecv.at[t, d, k - 1]
        return remote(
            src, zrecv.at[t, d, k], z_s.at[t, d, k], z_r.at[t, d, k], {"dp": zdev(1 if d else -1)}
        )

    def ring_start(t):
        for d in range(2):
            zsrc[t, d] = terms[t, :, owner(zcount(t, d), d, 0)].astype(BF)
            zcopy(t, d, 0).start()

    def ring_step(t, k):
        for d in range(2):
            n = zcount(t, d)
            if k < n:
                zcopy(t, d, k - 1).wait_recv()
                mine = terms[t, :, owner(n, d, k)]
                zrecv[t, d, k - 1] = (zrecv[t, d, k - 1].astype(F32) + mine).astype(BF)
                zcopy(t, d, k).start()

    def make_term(t):
        rows_of, code = (xg, cup) if t == 0 else (cg, cdn)
        for kb in range(4):
            r = mm(rows_of[kb].reshape(128, 768), code[...], TN)
            terms[t, kb] = r.reshape(zn, 64, 128)

    def codes():
        cup[...] = mm(ug[...], proj[0], NN).astype(BF)
        with scope("terms"):
            for t in range(2):
                make_term(t)
                ring_start(t)

    with scope("first0"):
        first(0)
    with scope("second0"):
        second(0)
    with scope("first1"):
        first(1)

    @pl.when(s == 0)
    def _():
        finish(0)
        codes()

    with scope("second1"):
        second(1)

    @pl.when(s > 0)
    def _():
        finish(0)
        finish(1)

        @pl.when(s == 3)
        def _():
            prep()

        codes()

    for k in range(1, 6):
        with scope("ringstep"):
            for t in range(2):
                ring_step(t, k)
        if k == 3:
            @pl.when(s == 0)
            def _():
                finish(1)

    def ycopy(t, k):
        return remote(
            ysend.at[t, k], yrecv.at[t, k], y_s.at[t, k], y_r.at[t, k], {"dp": ydev(k)}
        )

    with scope("ringlast"):
        for t in range(2):
            for d in range(2):
                zcopy(t, d, zcount(t, d) - 1).wait_recv()
            for k in (3, 2, 1, 0):
                yo = lax.rem(y + k, 4)
                r = terms[t, yo, z]
                for d in range(2):
                    r += zrecv[t, d, zcount(t, d) - 1, yo].astype(F32)
                if k:
                    ysend[t, k] = r.astype(BF)
                    ycopy(t, k).start()
                else:
                    ykeep[t] = r

    for t in range(2):
        grad = ykeep[t]
        with scope("ywait"):
            for k in (1, 2, 3):
                ycopy(t, k).wait_recv()
                grad += yrecv[t, k].astype(F32)
        new_first = 0.9 * m1[t] + 0.1 * grad
        new_second = 0.999 * m2[t] + 0.001 * grad * grad
        nfv[t] = new_first
        nsv[t] = new_second
        step = new_first / (jnp.sqrt(new_second) + 1e-08)
        high = step.astype(BF)
        low = (step - high.astype(F32)).astype(BF)
        delta = mm(high, proj[t], NT) + mm(low, proj[t], NT)
        (nup, ndown)[t][...] = (base[t] - 0.05 * delta).astype(BF)

    @pl.when(s == 3)
    def _():
        for u in range(2):
            for k in ORDER:
                gather_top(u, k).wait_send()

    @pl.when(s == 1)
    def _():
        for u in range(2):
            for k in ORDER:
                gather_cot(u, k).wait_send()

    @pl.when(odd)
    def _():
        for u in range(2):
            for k in range(4):
                cast_down(u, k).wait_send()

    @pl.when(s == 2)
    def _():
        for u in range(2):
            hop(u).wait_send()

    for k in ORDER:
        gather_in(k).wait_send()
        for u in range(2):
            scatter(u, k).wait_send()
            ycopy(u, k).wait_send()
    for t in range(2):
        for d in range(2):
            for k in range(zcount(t, d)):
                zcopy(t, d, k).wait_send()


def copy_kernel(*refs):
    half = len(refs) // 2
    sems = refs[-1]
    copies = [
        pltpu.make_async_copy(refs[i], refs[half + i], sems.at[i]) for i in range(half)
    ]
    for c in copies:
        c.start()
    for c in copies:
        c.wait()


def hand_out(*arrays):
    return pl.pallas_call(
        copy_kernel,
        out_shape=tuple(jax.ShapeDtypeStruct(a.shape, a.dtype) for a in arrays),
        in_specs=[pl.BlockSpec(memory_space=pl.ANY)] * len(arrays),
        out_specs=(pl.BlockSpec(memory_space=pl.ANY),) * len(arrays),
        scratch_shapes=[pltpu.SemaphoreType.DMA((len(arrays),))],
        compiler_params=pltpu.CompilerParams(vmem_limit_bytes=2 * 2**20),
        name="hand_out",
    )(*arrays)


def local(zn, inputs, gate_sums, top_grads, up_weight, down_weight, projectors, first_moment, second_moment):
    sds = jax.ShapeDtypeStruct
    any_spec = pl.BlockSpec(memory_space=pl.ANY)
    dma = pltpu.SemaphoreType.DMA
    og, nf, ns, nu, nd = pl.pallas_call(
        functools.partial(kernel, zn),
        out_shape=(
            pltpu.VMEM((2, 64, 768), BF),
            pltpu.VMEM((2, 64, 128), F32),
            pltpu.VMEM((2, 64, 128), F32),
            pltpu.VMEM((64, 816), BF),
            pltpu.VMEM((64, 816), BF),
        ),
        in_specs=[any_spec] * 8,
        out_specs=(pl.BlockSpec(memory_space=pltpu.VMEM),) * 5,
        scratch_shapes=[
            pltpu.VMEM((4, 816, 768), BF),
            pltpu.VMEM((4, 816, 768), BF),
            pltpu.VMEM((2, 816, 128), BF),
            pltpu.VMEM((2, 64, 816), BF),
            pltpu.VMEM((2, 64, 128), F32),
            pltpu.VMEM((2, 64, 128), F32),
            pltpu.VMEM((4, 2, 64, 768), BF),
            pltpu.VMEM((4, 2, 64, 768), BF),
            pltpu.VMEM((128, 816), F32),
            pltpu.VMEM((128, 816), F32),
            pltpu.VMEM((128, 816), BF),
            pltpu.VMEM((128, 816), BF),
            pltpu.VMEM((2, 4, 64, 768), BF),
            pltpu.VMEM((2, 4, 64, 768), BF),
            pltpu.VMEM((128, 128), BF),
            pltpu.VMEM((128, 128), BF),
            pltpu.VMEM((2, 4, zn, 64, 128), F32),
            pltpu.VMEM((2, 2, 4, 64, 128), BF),
            pltpu.VMEM((2, 2, 6, 4, 64, 128), BF),
            pltpu.VMEM((2, 4, 64, 128), BF),
            pltpu.VMEM((2, 4, 64, 128), BF),
            pltpu.VMEM((2, 64, 128), F32),
            pltpu.VMEM((2, 64, 816), F32),
            dma((6,)),
            dma((2, 4)),
            dma((2, 4)),
            dma((2, 4)),
            dma((2, 4)),
            dma((2,)),
            dma((2,)),
            dma((4,)),
            dma((4,)),
            dma((2, 4)),
            dma((2, 4)),
            dma((2, 2, 6)),
            dma((2, 2, 6)),
            dma((2, 4)),
            dma((2, 4)),
        ],
        compiler_params=pltpu.CompilerParams(
            collective_id=0, has_side_effects=True, vmem_limit_bytes=60 * 2**20
        ),
        name="relay",
    )(
        inputs[0],
        gate_sums[0],
        top_grads,
        jnp.swapaxes(up_weight[0], 0, 1),
        down_weight[0],
        projectors[0],
        jnp.swapaxes(first_moment[0, 0], 1, 2),
        jnp.swapaxes(second_moment[0, 0], 1, 2),
    )
    og, nf, ns, nu, nd = hand_out(og, nf, ns, nu, nd)
    return (
        og[None],
        jnp.swapaxes(nf, 1, 2)[None, None],
        jnp.swapaxes(ns, 1, 2)[None, None],
        nu[None],
        jnp.swapaxes(nd, 0, 1)[None],
    )


def solution(mesh):
    placed = (
        P("segment", None, "dp", "lane"),
        P("segment", None, "dp", "lane"),
        P(None, "dp", "lane"),
        P("segment", None, "lane"),
        P("segment", "lane", None),
        P("segment", None, "lane", None),
        P("segment", "lane", None, None, "dp"),
        P("segment", "lane", None, None, "dp"),
    )
    return jax.shard_map(
        functools.partial(local, mesh.shape["dp"] // 4),
        mesh=mesh,
        in_specs=placed,
        out_specs=(
            P("segment", None, "dp", "lane"),
            P("segment", "lane", None, None, "dp"),
            P("segment", "lane", None, None, "dp"),
            P("segment", "dp", "lane"),
            P("segment", "lane", "dp"),
        ),
        check_vma=False,
    )
```

```python
import functools

import jax
import jax.numpy as jnp
from jax import lax
from jax.experimental import pallas as pl
from jax.experimental.pallas import tpu as pltpu
from jax.sharding import PartitionSpec as P

MESH = pl.DeviceIdType.MESH
NT = (((1,), (1,)), ((), ()))
NN = (((1,), (0,)), ((), ()))
TN = (((0,), (0,)), ((), ()))
BF = jnp.bfloat16
F32 = jnp.float32
UNIT = 64


def loop(count, body):
    lax.fori_loop(0, count, lambda i, c: (body(i), c)[1], 0)


def gray(p):
    return p + p // 2 - 2 * (p // 3)


def mm(a, b, dims):
    return lax.dot_general(a, b, dims, preferred_element_type=F32)


def kernel(
    zn,
    x_hbm, gate_hbm, top_hbm, wu_hbm, wd_hbm, proj_hbm, m1_hbm, m2_hbm,
    og, nfv, nsv, nup, ndown,
    wu, wd, proj, gate, m1, m2,
    rows_in, act, acc, ug, hid, part, prs,
    code, terms, zsrc, zrecv, ysend, yrecv, ykeep,
    base,
    loc, wsem,
    ag_s, bc_s, ag_r, yh_s, yh_r, in_s, in_r, rs_s, rs_r, z_s, z_r, y_s, y_r,
):
    xg, cg = rows_in.at[0], rows_in.at[1]
    s = lax.axis_index("segment")
    l = lax.axis_index("lane")
    dp = lax.axis_index("dp")
    z = lax.rem(dp, zn)
    y = dp // zn
    odd = lax.rem(s, 2) == 1
    pair = s + 1 - 2 * lax.rem(s, 2)

    def lane(k):
        return lax.rem(l + k, 4)

    def zdev(k):
        return y * zn + lax.rem(z + k + zn, zn)

    def ydev(k):
        return lax.rem(y + k, 4) * zn + z

    gate_load = pltpu.make_async_copy(gate_hbm, gate, loc.at[0])
    top_load = pltpu.make_async_copy(top_hbm, cg.at[l], loc.at[1])
    late_loads = [
        pltpu.make_async_copy(x_hbm, xg.at[l], loc.at[2]),
        pltpu.make_async_copy(proj_hbm, proj, loc.at[3]),
        pltpu.make_async_copy(m1_hbm, m1, loc.at[4]),
        pltpu.make_async_copy(m2_hbm, m2, loc.at[5]),
    ]
    wd_loads = [
        pltpu.make_async_copy(wd_hbm.at[:, pl.ds(kb * 768, 768)], wd.at[kb], wsem.at[0, kb])
        for kb in range(4)
    ]
    wu_loads = [
        pltpu.make_async_copy(wu_hbm.at[:, pl.ds(kb * 768, 768)], wu.at[kb], wsem.at[1, kb])
        for kb in range(4)
    ]

    @pl.when(s == 3)
    def _():
        top_load.start()

    gate_load.start()
    for c in wd_loads + wu_loads + late_loads:
        c.start()

    barrier = pltpu.get_barrier_semaphore()

    def greet(dev):
        pl.semaphore_signal(barrier, inc=1, device_id=dev, device_id_type=MESH)

    for k in (1, 2, 3):
        greet({"lane": lane(k)})
        greet({"dp": ydev(k)})
    for k in range(4):
        greet({"segment": pair, "lane": lane(k)})
    greet({"segment": 3 - s})
    greet({"dp": zdev(1)})
    greet({"dp": zdev(-1)})
    pl.semaphore_wait(barrier, 13)

    def remote(src, dst, ss, rr, dev):
        return pltpu.make_async_remote_copy(
            src_ref=src, dst_ref=dst, send_sem=ss, recv_sem=rr, device_id=dev, device_id_type=MESH
        )

    def rows(u):
        return pl.ds(pl.multiple_of(u * UNIT, UNIT), UNIT)

    def gather_top(u, k):
        return remote(
            top_hbm.at[rows(u)], cg.at[l, rows(u)], ag_s.at[u, k], ag_r.at[u, k], {"lane": lane(k)}
        )

    def gather_cot(u, k):
        block = cg.at[l, rows(u)]
        return remote(block, block, ag_s.at[u, k], ag_r.at[u, k], {"lane": lane(k)})

    def gather_in(k):
        return remote(x_hbm, xg.at[l], in_s.at[k], in_r.at[k], {"lane": lane(k)})

    def cast_down(u, k):
        return remote(
            og.at[rows(u)],
            cg.at[l, rows(u)],
            bc_s.at[u, k],
            ag_r.at[u, k],
            {"segment": pair, "lane": lane(k)},
        )

    def hop(u):
        return remote(
            og.at[rows(u)], cg.at[l, rows(u)], yh_s.at[u], yh_r.at[u], {"segment": 3 - s}
        )

    def scatter(u, k):
        return remote(
            part.at[k, rows(u)], prs.at[k, rows(u)], rs_s.at[u, k], rs_r.at[u, k], {"lane": lane(k)}
        )

    ORDER = (2, 1, 3)
    count = 128 // UNIT

    @pl.when(s == 3)
    def _():
        for u in range(count):
            for k in ORDER:
                gather_top(u, k).start()

    @pl.when(s < 2)
    def _():
        for k in ORDER:
            gather_in(k).start()

    gate_load.wait()
    v = gate[...].astype(F32)
    act[...] = v / (1.0 + jnp.exp(-v))

    for c in wd_loads + wu_loads:
        c.wait()

    @pl.when(s == 3)
    def _():
        top_load.wait()

    def prep():
        for c in late_loads:
            c.wait()
        acc[...] = jnp.zeros_like(acc)

        def block(p):
            k = gray(p)
            kb = lane(4 - k)

            @pl.when(p > 0)
            def _():
                gather_in(k).wait_recv()

            acc[...] += mm(xg[kb], wu[kb], NT)

        loop(4, block)
        hid[...] = (acc[...] * act[...]).astype(BF)
        code[1] = mm(hid[...], proj[1], NN).astype(BF)

    @pl.when(s < 2)
    def _():
        prep()

    def first(u):
        @pl.when(s == 1)
        def _():
            hop(u).wait_recv()
            for k in ORDER:
                gather_cot(u, k).start()

        acc[0:UNIT, :] = jnp.zeros((UNIT, 816), F32)

        def block(p):
            k = gray(p)
            kb = lane(4 - k)

            @pl.when((p > 0) | jnp.logical_not(odd))
            def _():
                gather_cot(u, k).wait_recv()

            acc[0:UNIT, :] += mm(cg[kb, rows(u)], wd[kb], NT)

        loop(4, block)
        ug[rows(u), :] = (acc[0:UNIT, :] * act[rows(u), :]).astype(BF)

    def second(u):
        def block(p):
            k = gray(3 - p)
            part[k, rows(u)] = mm(ug[rows(u), :], wu[lane(k)], NN).astype(BF)

            @pl.when(k > 0)
            def _():
                scatter(u, k).start()

        loop(4, block)

    def finish(u):
        total = cg[l, rows(u)].astype(F32) + part[0, rows(u)].astype(F32)
        for k in (1, 3, 2):
            scatter(u, k).wait_recv()
            total += prs[k, rows(u)].astype(F32)
        og[rows(u)] = total.astype(BF)

        @pl.when(odd)
        def _():
            for k in (2, 1, 3, 0):
                cast_down(u, k).start()

        @pl.when(s == 2)
        def _():
            hop(u).start()

    def chain(c):
        t, d, h = c // 4, lax.rem(c // 2, 2), lax.rem(c, 2)
        steps = 5 + lax.rem(t + d + 1, 2)
        return t, d, h, steps

    def zcopy(c, k, src):
        d = lax.rem(c // 2, 2)
        return remote(
            src, zrecv.at[c, k], z_s.at[c, k], z_r.at[c, k], {"dp": zdev(2 * d - 1)}
        )

    def local_term(c, k):
        t, d, h, steps = chain(c)
        to = lax.rem(z + (2 * d - 1) * (steps - k) + zn, zn)
        return terms[t, pl.ds(2 * h, 2), to]

    def codes():
        code[0] = mm(ug[...], proj[0], NN).astype(BF)
        for t in range(2):
            def term(kb):
                r = mm(rows_in[t, kb], code[t], TN)
                terms[t, kb] = r.reshape(zn, 64, 128)

            loop(4, term)

            def start(i):
                c = 4 * t + i
                zsrc[c] = local_term(c, 0).astype(BF)
                zcopy(c, 0, zsrc.at[c]).start()

            loop(4, start)

    last = count - 1

    def unit(u):
        first(u)

        @pl.when((u == last) & (s == 0))
        def _():
            codes()

        second(u)

        @pl.when(u > 0)
        def _():
            finish(u - 1)

    loop(count, unit)

    @pl.when(s > 0)
    def _():
        finish(last)

        @pl.when(s > 1)
        def _():
            for k in ORDER:
                gather_in(k).start()
            prep()

        codes()

    pick = lax.broadcasted_iota(jnp.int32, (64, 128), 0) + 64 * lax.rem(z, 2)
    pick = (lax.broadcasted_iota(jnp.int32, (64, 128), 1) == pick).astype(BF)
    at = pl.ds(pl.multiple_of((z // 2) * 128, 128), 128)
    base[0] = mm(pick, wu[y, :, at], NT)
    base[1] = mm(pick, wd[y, :, at], NT)

    def ring_step(i):
        k = i + 1

        def move(c):
            steps = chain(c)[3]

            @pl.when(k < steps)
            def _():
                held = zrecv.at[c, k - 1]
                zcopy(c, k - 1, held).wait_recv()
                zrecv[c, k - 1] = (held[...].astype(F32) + local_term(c, k)).astype(BF)
                zcopy(c, k, held).start()

        loop(8, move)

        @pl.when((k == 2) & (s == 0))
        def _():
            finish(last)

    loop(5, ring_step)

    def ycopy(t, k):
        return remote(
            ysend.at[t, k], yrecv.at[t, k], y_s.at[t, k], y_r.at[t, k], {"dp": ydev(k)}
        )

    for t in range(2):
        for i in range(4):
            c = 4 * t + i
            zcopy(c, 4 if i // 2 != t else 5, zrecv.at[c, 0]).wait_recv()

        def share(i):
            k = 3 - i
            yo = lax.rem(y + k, 4)
            r = terms[t, yo, z]
            for d in range(2):
                c = (t * 2 + d) * 2 + yo // 2
                r += zrecv[c, 5 if t == d else 4, lax.rem(yo, 2)].astype(F32)

            @pl.when(k > 0)
            def _():
                ysend[t, k] = r.astype(BF)
                ycopy(t, k).start()

            @pl.when(k == 0)
            def _():
                ykeep[t] = r

        loop(4, share)

    for t in range(2):
        grad = ykeep[t]
        for k in (1, 2, 3):
            ycopy(t, k).wait_recv()
            grad += yrecv[t, k].astype(F32)
        new_first = 0.9 * m1[t] + 0.1 * grad
        new_second = 0.999 * m2[t] + 0.001 * grad * grad
        nfv[t] = new_first
        nsv[t] = new_second
        step = new_first / (jnp.sqrt(new_second) + 1e-08)
        high = step.astype(BF)
        low = (step - high.astype(F32)).astype(BF)
        delta = mm(high, proj[t], NT) + mm(low, proj[t], NT)
        (nup, ndown)[t][...] = (base[t] - 0.05 * delta).astype(BF)

    def drain_unit(u):
        @pl.when(s == 3)
        def _():
            for k in ORDER:
                gather_top(u, k).wait_send()

        @pl.when(s == 1)
        def _():
            for k in ORDER:
                gather_cot(u, k).wait_send()

        @pl.when(odd)
        def _():
            for k in range(4):
                cast_down(u, k).wait_send()

        @pl.when(s == 2)
        def _():
            hop(u).wait_send()

        for k in ORDER:
            scatter(u, k).wait_send()

    loop(count, drain_unit)
    for k in ORDER:
        gather_in(k).wait_send()
        for t in range(2):
            ycopy(t, k).wait_send()
    def drain(c):
        def sent(k):
            zcopy(c, k, zsrc.at[c]).wait_send()

        loop(5, sent)

        @pl.when(chain(c)[3] == 6)
        def _():
            sent(5)

    loop(8, drain)


def copy_kernel(*refs):
    half = len(refs) // 2
    sems = refs[-1]
    copies = [
        pltpu.make_async_copy(refs[i], refs[half + i], sems.at[i]) for i in range(half)
    ]
    for c in copies:
        c.start()
    for c in copies:
        c.wait()


def hand_out(*arrays):
    return pl.pallas_call(
        copy_kernel,
        out_shape=tuple(jax.ShapeDtypeStruct(a.shape, a.dtype) for a in arrays),
        in_specs=[pl.BlockSpec(memory_space=pl.ANY)] * len(arrays),
        out_specs=(pl.BlockSpec(memory_space=pl.ANY),) * len(arrays),
        scratch_shapes=[pltpu.SemaphoreType.DMA((len(arrays),))],
        compiler_params=pltpu.CompilerParams(vmem_limit_bytes=2 * 2**20),
        name="hand_out",
    )(*arrays)


def local(zn, inputs, gate_sums, top_grads, up_weight, down_weight, projectors, first_moment, second_moment):
    sds = jax.ShapeDtypeStruct
    any_spec = pl.BlockSpec(memory_space=pl.ANY)
    dma = pltpu.SemaphoreType.DMA
    count = 128 // UNIT
    og, nf, ns, nu, nd = pl.pallas_call(
        functools.partial(kernel, zn),
        out_shape=(
            pltpu.VMEM((128, 768), BF),
            pltpu.VMEM((2, 64, 128), F32),
            pltpu.VMEM((2, 64, 128), F32),
            pltpu.VMEM((64, 816), BF),
            pltpu.VMEM((64, 816), BF),
        ),
        in_specs=[any_spec] * 8,
        out_specs=(pl.BlockSpec(memory_space=pltpu.VMEM),) * 5,
        scratch_shapes=[
            pltpu.VMEM((4, 816, 768), BF),
            pltpu.VMEM((4, 816, 768), BF),
            pltpu.VMEM((2, 816, 128), BF),
            pltpu.VMEM((128, 816), BF),
            pltpu.VMEM((2, 64, 128), F32),
            pltpu.VMEM((2, 64, 128), F32),
            pltpu.VMEM((2, 4, 128, 768), BF),
            pltpu.VMEM((128, 816), F32),
            pltpu.VMEM((128, 816), F32),
            pltpu.VMEM((128, 816), BF),
            pltpu.VMEM((128, 816), BF),
            pltpu.VMEM((4, 128, 768), BF),
            pltpu.VMEM((4, 128, 768), BF),
            pltpu.VMEM((2, 128, 128), BF),
            pltpu.VMEM((2, 4, zn, 64, 128), F32),
            pltpu.VMEM((8, 2, 64, 128), BF),
            pltpu.VMEM((8, 6, 2, 64, 128), BF),
            pltpu.VMEM((2, 4, 64, 128), BF),
            pltpu.VMEM((2, 4, 64, 128), BF),
            pltpu.VMEM((2, 64, 128), F32),
            pltpu.VMEM((2, 64, 816), F32),
            dma((6,)),
            dma((2, 4)),
            dma((count, 4)),
            dma((count, 4)),
            dma((count, 4)),
            dma((count,)),
            dma((count,)),
            dma((4,)),
            dma((4,)),
            dma((count, 4)),
            dma((count, 4)),
            dma((8, 6)),
            dma((8, 6)),
            dma((2, 4)),
            dma((2, 4)),
        ],
        compiler_params=pltpu.CompilerParams(
            collective_id=0, has_side_effects=True, vmem_limit_bytes=60 * 2**20
        ),
        name="relay",
    )(
        inputs[0].reshape(128, 768),
        gate_sums[0].reshape(128, 816),
        top_grads.reshape(128, 768),
        jnp.swapaxes(up_weight[0], 0, 1),
        down_weight[0],
        projectors[0],
        jnp.swapaxes(first_moment[0, 0], 1, 2),
        jnp.swapaxes(second_moment[0, 0], 1, 2),
    )
    og, nf, ns, nu, nd = hand_out(og, nf, ns, nu, nd)
    return (
        og.reshape(1, 2, 64, 768),
        jnp.swapaxes(nf, 1, 2)[None, None],
        jnp.swapaxes(ns, 1, 2)[None, None],
        nu[None],
        jnp.swapaxes(nd, 0, 1)[None],
    )


def solution(mesh):
    placed = (
        P("segment", None, "dp", "lane"),
        P("segment", None, "dp", "lane"),
        P(None, "dp", "lane"),
        P("segment", None, "lane"),
        P("segment", "lane", None),
        P("segment", None, "lane", None),
        P("segment", "lane", None, None, "dp"),
        P("segment", "lane", None, None, "dp"),
    )
    return jax.shard_map(
        functools.partial(local, mesh.shape["dp"] // 4),
        mesh=mesh,
        in_specs=placed,
        out_specs=(
            P("segment", None, "dp", "lane"),
            P("segment", "lane", None, None, "dp"),
            P("segment", "lane", None, None, "dp"),
            P("segment", "dp", "lane"),
            P("segment", "lane", "dp"),
        ),
        check_vma=False,
    )
```

```python
import functools

import jax
import jax.numpy as jnp
from jax import lax
from jax.experimental import pallas as pl
from jax.experimental.pallas import tpu as pltpu
from jax.sharding import PartitionSpec as P

MESH = pl.DeviceIdType.MESH
NT = (((1,), (1,)), ((), ()))
NN = (((1,), (0,)), ((), ()))
TN = (((0,), (0,)), ((), ()))
BF = jnp.bfloat16
F32 = jnp.float32
UNIT = 64


def loop(count, body):
    lax.fori_loop(0, count, lambda i, c: (body(i), c)[1], 0)


def gray(p):
    return p + p // 2 - 2 * (p // 3)


def mm(a, b, dims):
    return lax.dot_general(a, b, dims, preferred_element_type=F32)


def kernel(
    zn,
    x_hbm, gate_hbm, top_hbm, wu_hbm, wd_hbm, proj_hbm, m1_hbm, m2_hbm,
    og, nfv, nsv, nup, ndown,
    wu, wd, proj, gate, m1, m2,
    rows_in, act, acc, ug, hid, part, prs,
    code, terms, zsrc, zrecv, ysend, yrecv, ykeep,
    base, proj2, turned,
    loc, wsem,
    ag_s, bc_s, ag_r, yh_s, yh_r, in_s, in_r, rs_s, rs_r, z_s, z_r, y_s, y_r, turn,
):
    xg, cg = rows_in.at[0], rows_in.at[1]
    s = lax.axis_index("segment")
    l = lax.axis_index("lane")
    dp = lax.axis_index("dp")
    z = lax.rem(dp, zn)
    y = dp // zn
    odd = lax.rem(s, 2) == 1
    pair = s + 1 - 2 * lax.rem(s, 2)

    def lane(k):
        return lax.rem(l + k, 4)

    def zdev(k):
        return y * zn + lax.rem(z + k + zn, zn)

    def ydev(k):
        return lax.rem(y + k, 4) * zn + z

    gate_load = pltpu.make_async_copy(gate_hbm, gate, loc.at[0])
    top_load = pltpu.make_async_copy(top_hbm, cg.at[l], loc.at[1])
    late_loads = [
        pltpu.make_async_copy(x_hbm, xg.at[l], loc.at[2]),
        pltpu.make_async_copy(proj_hbm, proj, loc.at[3]),
        pltpu.make_async_copy(m1_hbm, m1, loc.at[4]),
        pltpu.make_async_copy(m2_hbm, m2, loc.at[5]),
    ]
    wd_loads = [
        pltpu.make_async_copy(wd_hbm.at[:, pl.ds(kb * 768, 768)], wd.at[kb], wsem.at[0, kb])
        for kb in range(4)
    ]
    wu_loads = [
        pltpu.make_async_copy(wu_hbm.at[:, pl.ds(kb * 768, 768)], wu.at[kb], wsem.at[1, kb])
        for kb in range(4)
    ]

    @pl.when(s == 3)
    def _():
        top_load.start()

    gate_load.start()
    for c in wd_loads + wu_loads + late_loads:
        c.start()

    barrier = pltpu.get_barrier_semaphore()

    def greet(dev):
        pl.semaphore_signal(barrier, inc=1, device_id=dev, device_id_type=MESH)

    for k in (1, 2, 3):
        greet({"lane": lane(k)})
        greet({"dp": ydev(k)})
    for k in range(4):
        greet({"segment": pair, "lane": lane(k)})
    greet({"segment": 3 - s})
    greet({"dp": zdev(1)})
    greet({"dp": zdev(-1)})
    pl.semaphore_wait(barrier, 13)

    def remote(src, dst, ss, rr, dev):
        return pltpu.make_async_remote_copy(
            src_ref=src, dst_ref=dst, send_sem=ss, recv_sem=rr, device_id=dev, device_id_type=MESH
        )

    def rows(u):
        return pl.ds(pl.multiple_of(u * UNIT, UNIT), UNIT)

    def gather_top(u, k):
        return remote(
            top_hbm.at[rows(u)], cg.at[l, rows(u)], ag_s.at[u, k], ag_r.at[u, k], {"lane": lane(k)}
        )

    def half(u, h):
        return pl.ds(pl.multiple_of(u * UNIT + h * (UNIT // 2), UNIT // 2), UNIT // 2)

    def gather_cot(u, k, span=None):
        block = cg.at[l, rows(u) if span is None else span]
        return remote(block, block, ag_s.at[u, k], ag_r.at[u, k], {"lane": lane(k)})

    def gather_in(k):
        return remote(x_hbm, xg.at[l], in_s.at[k], in_r.at[k], {"lane": lane(k)})

    def cast_down(u, k):
        return remote(
            og.at[rows(u)],
            cg.at[l, rows(u)],
            bc_s.at[u, k],
            ag_r.at[u, k],
            {"segment": pair, "lane": lane(k)},
        )

    def hop(u, h):
        return remote(
            og.at[half(u, h)], cg.at[l, half(u, h)], yh_s.at[u, h], yh_r.at[u, h], {"segment": 3 - s}
        )

    def scatter(u, k):
        return remote(
            part.at[k, rows(u)], prs.at[k, rows(u)], rs_s.at[u, k], rs_r.at[u, k], {"lane": lane(k)}
        )

    ORDER = (1, 3, 2)
    count = 128 // UNIT

    @pl.when(s == 3)
    def _():
        for k in ORDER:
            gather_top(0, k).start()

    @pl.when(s < 2)
    def _():
        for k in ORDER:
            gather_in(k).start()

    gate_load.wait()
    v = gate[...].astype(F32)
    act[...] = v / (1.0 + jnp.exp(-v))

    for c in wd_loads + wu_loads:
        c.wait()

    @pl.when(s == 3)
    def _():
        for u in range(1, count):
            for k in ORDER:
                gather_top(u, k).start()
        top_load.wait()

    def prep():
        for c in late_loads:
            c.wait()
        acc[...] = jnp.zeros_like(acc)

        def block(p):
            k = gray(p)
            kb = lane(4 - k)

            @pl.when(p > 0)
            def _():
                gather_in(k).wait_recv()

            acc[...] += mm(xg[kb], wu[kb], NT)

        loop(4, block)
        hid[...] = (acc[...] * act[...]).astype(BF)
        code[1] = mm(hid[...], proj[1], NN).astype(BF)

    @pl.when(s < 2)
    def _():
        prep()

    @pl.when(s < 3)
    def _():
        def turn_block(kb):
            turned[kb] = wd[kb].T

        loop(4, turn_block)

    def first(u):
        @pl.when(s == 1)
        def _():
            for h in range(2):
                hop(u, h).wait_recv()
                for k in ORDER:
                    gather_cot(u, k, half(u, h)).start()

        acc[0:UNIT, :] = jnp.zeros((UNIT, 816), F32)

        def block(p):
            k = gray(p)
            kb = lane(4 - k)

            @pl.when((p > 0) | jnp.logical_not(odd))
            def _():
                gather_cot(u, k).wait_recv()

            @pl.when(s == 3)
            def _():
                acc[0:UNIT, :] += mm(cg[kb, rows(u)], wd[kb], NT)

            @pl.when(s < 3)
            def _():
                acc[0:UNIT, :] += mm(cg[kb, rows(u)], turned[kb], NN)

        loop(4, block)
        ug[rows(u), :] = (acc[0:UNIT, :] * act[rows(u), :]).astype(BF)

    def second(u):
        def block(p):
            k = gray(3 - p)
            part[k, rows(u)] = mm(ug[rows(u), :], wu[lane(k)], NN).astype(BF)

            @pl.when(k > 0)
            def _():
                scatter(u, k).start()

        loop(4, block)

    def finish(u):
        total = cg[l, rows(u)].astype(F32) + part[0, rows(u)].astype(F32)
        for k in (1, 3, 2):
            scatter(u, k).wait_recv()
            total += prs[k, rows(u)].astype(F32)
        og[rows(u)] = total.astype(BF)

        @pl.when(odd)
        def _():
            for k in (0, 1, 3, 2):
                cast_down(u, k).start()

        @pl.when(s == 2)
        def _():
            for h in range(2):
                hop(u, h).start()

    def chain(c):
        t, d, h = c // 4, lax.rem(c // 2, 2), lax.rem(c, 2)
        steps = 5 + lax.rem(t + d + 1, 2)
        return t, d, h, steps

    def zcopy(c, k, src):
        d = lax.rem(c // 2, 2)
        return remote(
            src, zrecv.at[c, k], z_s.at[c, k], z_r.at[c, k], {"dp": zdev(2 * d - 1)}
        )

    def local_term(c, k):
        t, d, h, steps = chain(c)
        to = lax.rem(z + (2 * d - 1) * (steps - k) + zn, zn)
        return terms[t, pl.ds(2 * h, 2), to]

    def codes():
        code[0] = mm(ug[...], proj[0], NN).astype(BF)
        for t in range(2):
            def term(kb):
                r = mm(rows_in[t, kb], code[t], TN)
                terms[t, kb] = r.reshape(zn, 64, 128)

            loop(4, term)

            def start(i):
                c = 4 * t + i
                zsrc[c] = local_term(c, 0).astype(BF)
                zcopy(c, 0, zsrc.at[c]).start()

            loop(4, start)

    last = count - 1

    def unit(u):
        first(u)

        @pl.when((u == last) & (s == 0))
        def _():
            codes()

        second(u)

        @pl.when(u > 0)
        def _():
            finish(u - 1)

    loop(count, unit)

    @pl.when(s > 0)
    def _():
        finish(last)

        @pl.when(s == 2)
        def _():
            pl.semaphore_signal(turn, inc=1, device_id={"segment": 3}, device_id_type=MESH)

        @pl.when(s == 3)
        def _():
            pl.semaphore_wait(turn, 1)

        @pl.when(s > 1)
        def _():
            for k in ORDER:
                gather_in(k).start()
            prep()

        codes()

    def ring_step(i):
        k = i + 1

        def move(c):
            steps = chain(c)[3]

            @pl.when(k < steps)
            def _():
                held = zrecv.at[c, k - 1]
                zcopy(c, k - 1, held).wait_recv()
                zrecv[c, k - 1] = (held[...].astype(F32) + local_term(c, k)).astype(BF)
                zcopy(c, k, held).start()

        loop(8, move)

    loop(5, ring_step)

    def ycopy(t, k):
        return remote(
            ysend.at[t, k], yrecv.at[t, k], y_s.at[t, k], y_r.at[t, k], {"dp": ydev(k)}
        )

    for t in range(2):
        for i in range(4):
            c = 4 * t + i
            zcopy(c, 4 if i // 2 != t else 5, zrecv.at[c, 0]).wait_recv()

        def share(i):
            k = 3 - i
            yo = lax.rem(y + k, 4)
            r = terms[t, yo, z]
            for d in range(2):
                c = (t * 2 + d) * 2 + yo // 2
                r += zrecv[c, 5 if t == d else 4, lax.rem(yo, 2)].astype(F32)

            @pl.when(k > 0)
            def _():
                ysend[t, k] = r.astype(BF)
                ycopy(t, k).start()

            @pl.when(k == 0)
            def _():
                ykeep[t] = r

        loop(4, share)

    pick = lax.broadcasted_iota(jnp.int32, (64, 128), 0) + 64 * lax.rem(z, 2)
    pick = (lax.broadcasted_iota(jnp.int32, (64, 128), 1) == pick).astype(BF)
    at = pl.ds(pl.multiple_of((z // 2) * 128, 128), 128)
    proj2[:, :, 0:128] = proj[...]
    proj2[:, :, 128:256] = proj[...]
    base[0] = mm(pick, wu[y, :, at], NT)
    base[1] = mm(pick, wd[y, :, at], NT)

    @pl.when(s == 0)
    def _():
        finish(last)

    for t in range(2):
        grad = ykeep[t]
        for k in (1, 2, 3):
            ycopy(t, k).wait_recv()
            grad += yrecv[t, k].astype(F32)
        new_first = 0.9 * m1[t] + 0.1 * grad
        new_second = 0.999 * m2[t] + 0.001 * grad * grad
        nfv[t] = new_first
        nsv[t] = new_second
        step = new_first / (jnp.sqrt(new_second) + 1e-08)
        high = step.astype(BF)
        low = (step - high.astype(F32)).astype(BF)
        delta = mm(jnp.concatenate([high, low], axis=1), proj2[t], NT)
        (nup, ndown)[t][...] = (base[t] - 0.05 * delta).astype(BF)

    def drain_unit(u):
        @pl.when(s == 3)
        def _():
            for k in ORDER:
                gather_top(u, k).wait_send()

        @pl.when(s == 1)
        def _():
            for k in ORDER:
                gather_cot(u, k).wait_send()

        @pl.when(odd)
        def _():
            for k in range(4):
                cast_down(u, k).wait_send()

        @pl.when(s == 2)
        def _():
            for h in range(2):
                hop(u, h).wait_send()

        for k in ORDER:
            scatter(u, k).wait_send()

    loop(count, drain_unit)
    for k in ORDER:
        gather_in(k).wait_send()
        for t in range(2):
            ycopy(t, k).wait_send()
    def drain(c):
        def sent(k):
            zcopy(c, k, zsrc.at[c]).wait_send()

        loop(5, sent)

        @pl.when(chain(c)[3] == 6)
        def _():
            sent(5)

    loop(8, drain)


def copy_kernel(*refs):
    half = len(refs) // 2
    sems = refs[-1]
    copies = [
        pltpu.make_async_copy(refs[i], refs[half + i], sems.at[i]) for i in range(half)
    ]
    for c in copies:
        c.start()
    for c in copies:
        c.wait()


def hand_out(*arrays):
    return pl.pallas_call(
        copy_kernel,
        out_shape=tuple(jax.ShapeDtypeStruct(a.shape, a.dtype) for a in arrays),
        in_specs=[pl.BlockSpec(memory_space=pl.ANY)] * len(arrays),
        out_specs=(pl.BlockSpec(memory_space=pl.ANY),) * len(arrays),
        scratch_shapes=[pltpu.SemaphoreType.DMA((len(arrays),))],
        compiler_params=pltpu.CompilerParams(vmem_limit_bytes=2 * 2**20),
        name="hand_out",
    )(*arrays)


def local(zn, inputs, gate_sums, top_grads, up_weight, down_weight, projectors, first_moment, second_moment):
    sds = jax.ShapeDtypeStruct
    any_spec = pl.BlockSpec(memory_space=pl.ANY)
    dma = pltpu.SemaphoreType.DMA
    count = 128 // UNIT
    og, nf, ns, nu, nd = pl.pallas_call(
        functools.partial(kernel, zn),
        out_shape=(
            pltpu.VMEM((128, 768), BF),
            pltpu.VMEM((2, 64, 128), F32),
            pltpu.VMEM((2, 64, 128), F32),
            pltpu.VMEM((64, 816), BF),
            pltpu.VMEM((64, 816), BF),
        ),
        in_specs=[any_spec] * 8,
        out_specs=(pl.BlockSpec(memory_space=pltpu.VMEM),) * 5,
        scratch_shapes=[
            pltpu.VMEM((4, 816, 768), BF),
            pltpu.VMEM((4, 816, 768), BF),
            pltpu.VMEM((2, 816, 128), BF),
            pltpu.VMEM((128, 816), BF),
            pltpu.VMEM((2, 64, 128), F32),
            pltpu.VMEM((2, 64, 128), F32),
            pltpu.VMEM((2, 4, 128, 768), BF),
            pltpu.VMEM((128, 816), F32),
            pltpu.VMEM((128, 816), F32),
            pltpu.VMEM((128, 816), BF),
            pltpu.VMEM((128, 816), BF),
            pltpu.VMEM((4, 128, 768), BF),
            pltpu.VMEM((4, 128, 768), BF),
            pltpu.VMEM((2, 128, 128), BF),
            pltpu.VMEM((2, 4, zn, 64, 128), F32),
            pltpu.VMEM((8, 2, 64, 128), BF),
            pltpu.VMEM((8, 6, 2, 64, 128), BF),
            pltpu.VMEM((2, 4, 64, 128), BF),
            pltpu.VMEM((2, 4, 64, 128), BF),
            pltpu.VMEM((2, 64, 128), F32),
            pltpu.VMEM((2, 64, 816), F32),
            pltpu.VMEM((2, 816, 256), BF),
            pltpu.VMEM((4, 768, 816), BF),
            dma((6,)),
            dma((2, 4)),
            dma((count, 4)),
            dma((count, 4)),
            dma((count, 4)),
            dma((count, 2)),
            dma((count, 2)),
            dma((4,)),
            dma((4,)),
            dma((count, 4)),
            dma((count, 4)),
            dma((8, 6)),
            dma((8, 6)),
            dma((2, 4)),
            dma((2, 4)),
            pltpu.SemaphoreType.REGULAR,
        ],
        compiler_params=pltpu.CompilerParams(
            collective_id=0, has_side_effects=True, vmem_limit_bytes=60 * 2**20
        ),
        name="relay",
    )(
        inputs[0].reshape(128, 768),
        gate_sums[0].reshape(128, 816),
        top_grads.reshape(128, 768),
        jnp.swapaxes(up_weight[0], 0, 1),
        down_weight[0],
        projectors[0],
        jnp.swapaxes(first_moment[0, 0], 1, 2),
        jnp.swapaxes(second_moment[0, 0], 1, 2),
    )
    og, nf, ns, nu, nd = hand_out(og, nf, ns, nu, nd)
    return (
        og.reshape(1, 2, 64, 768),
        jnp.swapaxes(nf, 1, 2)[None, None],
        jnp.swapaxes(ns, 1, 2)[None, None],
        nu[None],
        jnp.swapaxes(nd, 0, 1)[None],
    )


def solution(mesh):
    placed = (
        P("segment", None, "dp", "lane"),
        P("segment", None, "dp", "lane"),
        P(None, "dp", "lane"),
        P("segment", None, "lane"),
        P("segment", "lane", None),
        P("segment", None, "lane", None),
        P("segment", "lane", None, None, "dp"),
        P("segment", "lane", None, None, "dp"),
    )
    return jax.shard_map(
        functools.partial(local, mesh.shape["dp"] // 4),
        mesh=mesh,
        in_specs=placed,
        out_specs=(
            P("segment", None, "dp", "lane"),
            P("segment", "lane", None, None, "dp"),
            P("segment", "lane", None, None, "dp"),
            P("segment", "dp", "lane"),
            P("segment", "lane", "dp"),
        ),
        check_vma=False,
    )
```

```python
import functools

import jax
import jax.numpy as jnp
from jax import lax
from jax.experimental import pallas as pl
from jax.experimental.pallas import tpu as pltpu
from jax.sharding import PartitionSpec as P

MESH = pl.DeviceIdType.MESH
NT = (((1,), (1,)), ((), ()))
NN = (((1,), (0,)), ((), ()))
TN = (((0,), (0,)), ((), ()))
BF = jnp.bfloat16
F32 = jnp.float32
UNIT = 64


def loop(count, body):
    lax.fori_loop(0, count, lambda i, c: (body(i), c)[1], 0)


def gray(p):
    return p + p // 2 - 2 * (p // 3)


def mm(a, b, dims):
    return lax.dot_general(a, b, dims, preferred_element_type=F32)


def kernel(
    zn,
    x_hbm, gate_hbm, top_hbm, wu_hbm, wd_hbm, proj_hbm, m1_hbm, m2_hbm,
    og, nfv, nsv, nup, ndown,
    wu, wd, proj, gate, m1, m2,
    rows_in, act, acc, ug, hid, part, prs,
    code, terms, zsrc, zrecv, ysend, yrecv, ykeep,
    base, proj2, turned,
    loc, wsem,
    ag_s, bc_s, ag_r, yh_s, yh_r, in_s, in_r, rs_s, rs_r, z_s, z_r, y_s, y_r, turn,
):
    xg, cg = rows_in.at[0], rows_in.at[1]
    s = lax.axis_index("segment")
    l = lax.axis_index("lane")
    dp = lax.axis_index("dp")
    z = lax.rem(dp, zn)
    y = dp // zn
    odd = lax.rem(s, 2) == 1
    pair = s + 1 - 2 * lax.rem(s, 2)

    def lane(k):
        return lax.rem(l + k, 4)

    def zdev(k):
        return y * zn + lax.rem(z + k + zn, zn)

    def ydev(k):
        return lax.rem(y + k, 4) * zn + z

    gate_load = pltpu.make_async_copy(gate_hbm, gate, loc.at[0])
    top_load = pltpu.make_async_copy(top_hbm, cg.at[l], loc.at[1])
    late_loads = [
        pltpu.make_async_copy(x_hbm, xg.at[l], loc.at[2]),
        pltpu.make_async_copy(proj_hbm, proj, loc.at[3]),
        pltpu.make_async_copy(m1_hbm, m1, loc.at[4]),
        pltpu.make_async_copy(m2_hbm, m2, loc.at[5]),
    ]
    wd_loads = [
        pltpu.make_async_copy(wd_hbm.at[:, pl.ds(kb * 768, 768)], wd.at[kb], wsem.at[0, kb])
        for kb in range(4)
    ]
    wu_loads = [
        pltpu.make_async_copy(wu_hbm.at[:, pl.ds(kb * 768, 768)], wu.at[kb], wsem.at[1, kb])
        for kb in range(4)
    ]

    @pl.when(s == 3)
    def _():
        top_load.start()

    gate_load.start()
    for c in wd_loads + wu_loads + late_loads:
        c.start()

    barrier = pltpu.get_barrier_semaphore()

    def greet(dev):
        pl.semaphore_signal(barrier, inc=1, device_id=dev, device_id_type=MESH)

    for k in (1, 2, 3):
        greet({"lane": lane(k)})
        greet({"dp": ydev(k)})
    for k in range(4):
        greet({"segment": pair, "lane": lane(k)})
    across = (s == 1) | (s == 2)

    @pl.when(across)
    def _():
        greet({"segment": 3 - s})

    greet({"dp": zdev(1)})
    greet({"dp": zdev(-1)})
    pl.semaphore_wait(barrier, 12 + across.astype(jnp.int32))

    def remote(src, dst, ss, rr, dev):
        return pltpu.make_async_remote_copy(
            src_ref=src, dst_ref=dst, send_sem=ss, recv_sem=rr, device_id=dev, device_id_type=MESH
        )

    def rows(u):
        return pl.ds(pl.multiple_of(u * UNIT, UNIT), UNIT)

    def gather_top(u, k):
        return remote(
            top_hbm.at[rows(u)], cg.at[l, rows(u)], ag_s.at[u, k], ag_r.at[u, k], {"lane": lane(k)}
        )

    def half(u, h):
        return pl.ds(pl.multiple_of(u * UNIT + h * (UNIT // 2), UNIT // 2), UNIT // 2)

    def gather_cot(u, k, span=None):
        block = cg.at[l, rows(u) if span is None else span]
        return remote(block, block, ag_s.at[u, k], ag_r.at[u, k], {"lane": lane(k)})

    def gather_in(k):
        return remote(x_hbm, xg.at[l], in_s.at[k], in_r.at[k], {"lane": lane(k)})

    def cast_down(u, k):
        return remote(
            og.at[rows(u)],
            cg.at[l, rows(u)],
            bc_s.at[u, k],
            ag_r.at[u, k],
            {"segment": pair, "lane": lane(k)},
        )

    def hop(u, h):
        return remote(
            og.at[half(u, h)], cg.at[l, half(u, h)], yh_s.at[u, h], yh_r.at[u, h], {"segment": 3 - s}
        )

    def scatter(u, k):
        return remote(
            part.at[k, rows(u)], prs.at[k, rows(u)], rs_s.at[u, k], rs_r.at[u, k], {"lane": lane(k)}
        )

    ORDER = (1, 3, 2)
    count = 128 // UNIT

    @pl.when(s == 3)
    def _():
        for k in ORDER:
            gather_top(0, k).start()

    @pl.when(s < 2)
    def _():
        for k in ORDER:
            gather_in(k).start()

    gate_load.wait()
    v = gate[...].astype(F32)
    act[...] = v / (1.0 + jnp.exp(-v))

    @pl.when(s == 3)
    def _():
        for u in range(1, count):
            for k in ORDER:
                gather_top(u, k).start()
        top_load.wait()

    for c in wd_loads:
        c.wait()

    def turn_block(kb):
        turned[kb] = wd[kb].T

    loop(4, turn_block)
    for c in wu_loads:
        c.wait()

    def prep():
        for c in late_loads:
            c.wait()
        acc[...] = jnp.zeros_like(acc)

        def block(p):
            k = gray(p)
            kb = lane(4 - k)

            @pl.when(p > 0)
            def _():
                gather_in(k).wait_recv()

            acc[...] += mm(xg[kb], wu[kb], NT)

        loop(4, block)
        hid[...] = (acc[...] * act[...]).astype(BF)
        code[1] = mm(hid[...], proj[1], NN).astype(BF)

    @pl.when(s < 2)
    def _():
        prep()

    def first(u):
        @pl.when(s == 1)
        def _():
            for h in range(2):
                hop(u, h).wait_recv()
                for k in ORDER:
                    gather_cot(u, k, half(u, h)).start()

        acc[0:UNIT, :] = jnp.zeros((UNIT, 816), F32)

        def block(p):
            k = gray(p)
            kb = lane(4 - k)

            @pl.when((p > 0) | jnp.logical_not(odd))
            def _():
                gather_cot(u, k).wait_recv()

            acc[0:UNIT, :] += mm(cg[kb, rows(u)], turned[kb], NN)

        loop(4, block)
        ug[rows(u), :] = (acc[0:UNIT, :] * act[rows(u), :]).astype(BF)

    def second(u):
        def block(p):
            k = gray(3 - p)
            part[k, rows(u)] = mm(ug[rows(u), :], wu[lane(k)], NN).astype(BF)

            @pl.when(k > 0)
            def _():
                scatter(u, k).start()

        loop(4, block)

    def finish(u):
        total = cg[l, rows(u)].astype(F32) + part[0, rows(u)].astype(F32)
        for k in (1, 3, 2):
            scatter(u, k).wait_recv()
            total += prs[k, rows(u)].astype(F32)
        og[rows(u)] = total.astype(BF)

        @pl.when(odd)
        def _():
            for k in (0, 1, 3, 2):
                cast_down(u, k).start()

        @pl.when(s == 2)
        def _():
            for h in range(2):
                hop(u, h).start()

    def chain(c):
        t, d, h = c // 4, lax.rem(c // 2, 2), lax.rem(c, 2)
        steps = 5 + lax.rem(t + d + 1, 2)
        return t, d, h, steps

    def zcopy(c, k, src):
        d = lax.rem(c // 2, 2)
        return remote(
            src, zrecv.at[c, k], z_s.at[c, k], z_r.at[c, k], {"dp": zdev(2 * d - 1)}
        )

    def local_term(c, k):
        t, d, h, steps = chain(c)
        to = lax.rem(z + (2 * d - 1) * (steps - k) + zn, zn)
        return terms[t, pl.ds(2 * h, 2), to]

    def codes():
        code[0] = mm(ug[...], proj[0], NN).astype(BF)
        for t in range(2):
            def term(kb):
                r = mm(rows_in[t, kb], code[t], TN)
                terms[t, kb] = r.reshape(zn, 64, 128)

            loop(4, term)

            def start(i):
                c = 4 * t + i
                zsrc[c] = local_term(c, 0).astype(BF)
                zcopy(c, 0, zsrc.at[c]).start()

            loop(4, start)

    last = count - 1

    def unit(u):
        first(u)

        @pl.when((u == last) & (s == 0))
        def _():
            codes()

        second(u)

        @pl.when(u > 0)
        def _():
            finish(u - 1)

    loop(count, unit)

    @pl.when(s > 0)
    def _():
        finish(last)

        @pl.when(s == 2)
        def _():
            pl.semaphore_signal(turn, inc=1, device_id={"segment": 3}, device_id_type=MESH)

        @pl.when(s == 3)
        def _():
            pl.semaphore_wait(turn, 1)

        @pl.when(s > 1)
        def _():
            for k in ORDER:
                gather_in(k).start()
            prep()

        codes()

    def ring_step(i):
        k = i + 1

        def move(c):
            steps = chain(c)[3]

            @pl.when(k < steps)
            def _():
                held = zrecv.at[c, k - 1]
                zcopy(c, k - 1, held).wait_recv()
                zrecv[c, k - 1] = (held[...].astype(F32) + local_term(c, k)).astype(BF)
                zcopy(c, k, held).start()

        loop(8, move)

    loop(5, ring_step)

    def ycopy(t, k):
        return remote(
            ysend.at[t, k], yrecv.at[t, k], y_s.at[t, k], y_r.at[t, k], {"dp": ydev(k)}
        )

    for t in range(2):
        for i in range(4):
            c = 4 * t + i
            zcopy(c, 4 if i // 2 != t else 5, zrecv.at[c, 0]).wait_recv()

        def share(i):
            k = 3 - i
            yo = lax.rem(y + k, 4)
            r = terms[t, yo, z]
            for d in range(2):
                c = (t * 2 + d) * 2 + yo // 2
                r += zrecv[c, 5 if t == d else 4, lax.rem(yo, 2)].astype(F32)

            @pl.when(k > 0)
            def _():
                ysend[t, k] = r.astype(BF)
                ycopy(t, k).start()

            @pl.when(k == 0)
            def _():
                ykeep[t] = r

        loop(4, share)

    pick = lax.broadcasted_iota(jnp.int32, (64, 128), 0) + 64 * lax.rem(z, 2)
    pick = (lax.broadcasted_iota(jnp.int32, (64, 128), 1) == pick).astype(BF)
    at = pl.ds(pl.multiple_of((z // 2) * 128, 128), 128)
    proj2[:, :, 0:128] = proj[...]
    proj2[:, :, 128:256] = proj[...]
    base[0] = mm(pick, wu[y, :, at], NT)
    base[1] = mm(pick, wd[y, :, at], NT)

    @pl.when(s == 0)
    def _():
        finish(last)

    for t in range(2):
        grad = ykeep[t]
        for k in (1, 2, 3):
            ycopy(t, k).wait_recv()
            grad += yrecv[t, k].astype(F32)
        new_first = 0.9 * m1[t] + 0.1 * grad
        new_second = 0.999 * m2[t] + 0.001 * grad * grad
        nfv[t] = new_first
        nsv[t] = new_second
        step = new_first / (jnp.sqrt(new_second) + 1e-08)
        high = step.astype(BF)
        low = (step - high.astype(F32)).astype(BF)
        delta = mm(jnp.concatenate([high, low], axis=1), proj2[t], NT)
        (nup, ndown)[t][...] = (base[t] - 0.05 * delta).astype(BF)

    def drain_unit(u):
        @pl.when(s == 3)
        def _():
            for k in ORDER:
                gather_top(u, k).wait_send()

        @pl.when(s == 1)
        def _():
            for k in ORDER:
                gather_cot(u, k).wait_send()

        @pl.when(odd)
        def _():
            for k in range(4):
                cast_down(u, k).wait_send()

        @pl.when(s == 2)
        def _():
            for h in range(2):
                hop(u, h).wait_send()

        for k in ORDER:
            scatter(u, k).wait_send()

    loop(count, drain_unit)
    for k in ORDER:
        gather_in(k).wait_send()
        for t in range(2):
            ycopy(t, k).wait_send()
    def drain(c):
        def sent(k):
            zcopy(c, k, zsrc.at[c]).wait_send()

        loop(5, sent)

        @pl.when(chain(c)[3] == 6)
        def _():
            sent(5)

    loop(8, drain)


def copy_kernel(*refs):
    half = len(refs) // 2
    sems = refs[-1]
    copies = [
        pltpu.make_async_copy(refs[i], refs[half + i], sems.at[i]) for i in range(half)
    ]
    for c in copies:
        c.start()
    for c in copies:
        c.wait()


def hand_out(*arrays):
    return pl.pallas_call(
        copy_kernel,
        out_shape=tuple(jax.ShapeDtypeStruct(a.shape, a.dtype) for a in arrays),
        in_specs=[pl.BlockSpec(memory_space=pl.ANY)] * len(arrays),
        out_specs=(pl.BlockSpec(memory_space=pl.ANY),) * len(arrays),
        scratch_shapes=[pltpu.SemaphoreType.DMA((len(arrays),))],
        compiler_params=pltpu.CompilerParams(vmem_limit_bytes=2 * 2**20),
        name="hand_out",
    )(*arrays)


def local(zn, inputs, gate_sums, top_grads, up_weight, down_weight, projectors, first_moment, second_moment):
    sds = jax.ShapeDtypeStruct
    any_spec = pl.BlockSpec(memory_space=pl.ANY)
    dma = pltpu.SemaphoreType.DMA
    count = 128 // UNIT
    og, nf, ns, nu, nd = pl.pallas_call(
        functools.partial(kernel, zn),
        out_shape=(
            pltpu.VMEM((128, 768), BF),
            pltpu.VMEM((2, 64, 128), F32),
            pltpu.VMEM((2, 64, 128), F32),
            pltpu.VMEM((64, 816), BF),
            pltpu.VMEM((64, 816), BF),
        ),
        in_specs=[any_spec] * 8,
        out_specs=(pl.BlockSpec(memory_space=pltpu.VMEM),) * 5,
        scratch_shapes=[
            pltpu.VMEM((4, 816, 768), BF),
            pltpu.VMEM((4, 816, 768), BF),
            pltpu.VMEM((2, 816, 128), BF),
            pltpu.VMEM((128, 816), BF),
            pltpu.VMEM((2, 64, 128), F32),
            pltpu.VMEM((2, 64, 128), F32),
            pltpu.VMEM((2, 4, 128, 768), BF),
            pltpu.VMEM((128, 816), F32),
            pltpu.VMEM((128, 816), F32),
            pltpu.VMEM((128, 816), BF),
            pltpu.VMEM((128, 816), BF),
            pltpu.VMEM((4, 128, 768), BF),
            pltpu.VMEM((4, 128, 768), BF),
            pltpu.VMEM((2, 128, 128), BF),
            pltpu.VMEM((2, 4, zn, 64, 128), F32),
            pltpu.VMEM((8, 2, 64, 128), BF),
            pltpu.VMEM((8, 6, 2, 64, 128), BF),
            pltpu.VMEM((2, 4, 64, 128), BF),
            pltpu.VMEM((2, 4, 64, 128), BF),
            pltpu.VMEM((2, 64, 128), F32),
            pltpu.VMEM((2, 64, 816), F32),
            pltpu.VMEM((2, 816, 256), BF),
            pltpu.VMEM((4, 768, 816), BF),
            dma((6,)),
            dma((2, 4)),
            dma((count, 4)),
            dma((count, 4)),
            dma((count, 4)),
            dma((count, 2)),
            dma((count, 2)),
            dma((4,)),
            dma((4,)),
            dma((count, 4)),
            dma((count, 4)),
            dma((8, 6)),
            dma((8, 6)),
            dma((2, 4)),
            dma((2, 4)),
            pltpu.SemaphoreType.REGULAR,
        ],
        compiler_params=pltpu.CompilerParams(
            collective_id=0, has_side_effects=True, vmem_limit_bytes=60 * 2**20
        ),
        name="relay",
    )(
        inputs[0].reshape(128, 768),
        gate_sums[0].reshape(128, 816),
        top_grads.reshape(128, 768),
        jnp.swapaxes(up_weight[0], 0, 1),
        down_weight[0],
        projectors[0],
        jnp.swapaxes(first_moment[0, 0], 1, 2),
        jnp.swapaxes(second_moment[0, 0], 1, 2),
    )
    og, nf, ns, nu, nd = hand_out(og, nf, ns, nu, nd)
    return (
        og.reshape(1, 2, 64, 768),
        jnp.swapaxes(nf, 1, 2)[None, None],
        jnp.swapaxes(ns, 1, 2)[None, None],
        nu[None],
        jnp.swapaxes(nd, 0, 1)[None],
    )


def solution(mesh):
    placed = (
        P("segment", None, "dp", "lane"),
        P("segment", None, "dp", "lane"),
        P(None, "dp", "lane"),
        P("segment", None, "lane"),
        P("segment", "lane", None),
        P("segment", None, "lane", None),
        P("segment", "lane", None, None, "dp"),
        P("segment", "lane", None, None, "dp"),
    )
    return jax.shard_map(
        functools.partial(local, mesh.shape["dp"] // 4),
        mesh=mesh,
        in_specs=placed,
        out_specs=(
            P("segment", None, "dp", "lane"),
            P("segment", "lane", None, None, "dp"),
            P("segment", "lane", None, None, "dp"),
            P("segment", "dp", "lane"),
            P("segment", "lane", "dp"),
        ),
        check_vma=False,
    )
```

```python
import functools

import jax
import jax.numpy as jnp
from jax import lax
from jax.experimental import pallas as pl
from jax.experimental.pallas import tpu as pltpu
from jax.sharding import PartitionSpec as P

MESH = pl.DeviceIdType.MESH
NT = (((1,), (1,)), ((), ()))
NN = (((1,), (0,)), ((), ()))
TN = (((0,), (0,)), ((), ()))
BF = jnp.bfloat16
F32 = jnp.float32
UNIT = 64


def loop(count, body):
    lax.fori_loop(0, count, lambda i, c: (body(i), c)[1], 0)


def gray(p):
    return p + p // 2 - 2 * (p // 3)


def mm(a, b, dims):
    return lax.dot_general(a, b, dims, preferred_element_type=F32)


def kernel(
    zn,
    x_hbm, gate_hbm, top_hbm, wu_hbm, wd_hbm, proj_hbm, m1_hbm, m2_hbm,
    og, nfv, nsv, nup, ndown,
    wu, wd, proj, gate, m1, m2,
    rows_in, act, acc, ug, hid, part, prs,
    code, terms, zsrc, zrecv, ysend, yrecv, ykeep,
    base, proj2, turned,
    loc, wsem,
    ag_s, bc_s, ag_r, yh_s, yh_r, in_s, in_r, rs_s, rs_r, z_s, z_r, y_s, y_r, turn,
):
    xg, cg = rows_in.at[0], rows_in.at[1]
    s = lax.axis_index("segment")
    l = lax.axis_index("lane")
    dp = lax.axis_index("dp")
    z = lax.rem(dp, zn)
    y = dp // zn
    odd = lax.rem(s, 2) == 1
    pair = s + 1 - 2 * lax.rem(s, 2)

    def lane(k):
        return lax.rem(l + k, 4)

    def zdev(k):
        return y * zn + lax.rem(z + k + zn, zn)

    def ydev(k):
        return lax.rem(y + k, 4) * zn + z

    gate_load = pltpu.make_async_copy(gate_hbm, gate, loc.at[0])
    top_load = pltpu.make_async_copy(top_hbm, cg.at[l], loc.at[1])
    late_loads = [
        pltpu.make_async_copy(x_hbm, xg.at[l], loc.at[2]),
        pltpu.make_async_copy(proj_hbm, proj, loc.at[3]),
        pltpu.make_async_copy(m1_hbm, m1, loc.at[4]),
        pltpu.make_async_copy(m2_hbm, m2, loc.at[5]),
    ]
    wd_loads = [
        pltpu.make_async_copy(wd_hbm.at[:, pl.ds(kb * 768, 768)], wd.at[kb], wsem.at[0, kb])
        for kb in range(4)
    ]
    wu_loads = [
        pltpu.make_async_copy(wu_hbm.at[:, pl.ds(kb * 768, 768)], wu.at[kb], wsem.at[1, kb])
        for kb in range(4)
    ]

    @pl.when(s == 3)
    def _():
        top_load.start()

    gate_load.start()
    for c in wd_loads + wu_loads + late_loads:
        c.start()

    barrier = pltpu.get_barrier_semaphore()

    def greet(dev):
        pl.semaphore_signal(barrier, inc=1, device_id=dev, device_id_type=MESH)

    for k in (1, 2, 3):
        greet({"lane": lane(k)})
        greet({"dp": ydev(k)})
    for k in range(4):
        greet({"segment": pair, "lane": lane(k)})
    across = (s == 1) | (s == 2)

    @pl.when(across)
    def _():
        greet({"segment": 3 - s})

    greet({"dp": zdev(1)})
    greet({"dp": zdev(-1)})
    pl.semaphore_wait(barrier, 12 + across.astype(jnp.int32))

    def remote(src, dst, ss, rr, dev):
        return pltpu.make_async_remote_copy(
            src_ref=src, dst_ref=dst, send_sem=ss, recv_sem=rr, device_id=dev, device_id_type=MESH
        )

    def rows(u):
        return pl.ds(pl.multiple_of(u * UNIT, UNIT), UNIT)

    def gather_top(u, k):
        return remote(
            top_hbm.at[rows(u)], cg.at[l, rows(u)], ag_s.at[u, k], ag_r.at[u, k], {"lane": lane(k)}
        )

    def half(u, h):
        return pl.ds(pl.multiple_of(u * UNIT + h * (UNIT // 2), UNIT // 2), UNIT // 2)

    def gather_cot(u, k, span=None):
        block = cg.at[l, rows(u) if span is None else span]
        return remote(block, block, ag_s.at[u, k], ag_r.at[u, k], {"lane": lane(k)})

    def gather_in(k):
        return remote(x_hbm, xg.at[l], in_s.at[k], in_r.at[k], {"lane": lane(k)})

    def cast_down(u, k):
        return remote(
            og.at[rows(u)],
            cg.at[l, rows(u)],
            bc_s.at[u, k],
            ag_r.at[u, k],
            {"segment": pair, "lane": lane(k)},
        )

    def hop(u, h):
        return remote(
            og.at[half(u, h)], cg.at[l, half(u, h)], yh_s.at[u, h], yh_r.at[u, h], {"segment": 3 - s}
        )

    def scatter(u, k):
        return remote(
            part.at[k, rows(u)], prs.at[k, rows(u)], rs_s.at[u, k], rs_r.at[u, k], {"lane": lane(k)}
        )

    ORDER = (1, 3, 2)
    count = 128 // UNIT

    @pl.when(s == 3)
    def _():
        for k in ORDER:
            gather_top(0, k).start()

    @pl.when(s < 2)
    def _():
        for k in ORDER:
            gather_in(k).start()

    gate_load.wait()
    v = gate[...].astype(F32)
    act[...] = v / (1.0 + jnp.exp(-v))

    @pl.when(s == 3)
    def _():
        for u in range(1, count):
            for k in ORDER:
                gather_top(u, k).start()
        top_load.wait()

    for c in wd_loads:
        c.wait()

    def turn_block(kb):
        turned[kb] = wd[kb].T

    loop(4, turn_block)
    for c in wu_loads:
        c.wait()

    def prep():
        for c in late_loads:
            c.wait()
        acc[...] = jnp.zeros_like(acc)

        def block(p):
            k = gray(p)
            kb = lane(4 - k)

            @pl.when(p > 0)
            def _():
                gather_in(k).wait_recv()

            acc[...] += mm(xg[kb], wu[kb], NT)

        loop(4, block)
        hid[...] = (acc[...] * act[...]).astype(BF)
        code[1] = mm(hid[...], proj[1], NN).astype(BF)

    @pl.when(s < 2)
    def _():
        prep()

    def first(u):
        @pl.when(s == 1)
        def _():
            for h in range(2):
                hop(u, h).wait_recv()
                for k in ORDER:
                    gather_cot(u, k, half(u, h)).start()

        acc[0:UNIT, :] = jnp.zeros((UNIT, 816), F32)

        def block(p):
            k = gray(p)
            kb = lane(4 - k)

            @pl.when((p > 0) | jnp.logical_not(odd))
            def _():
                gather_cot(u, k).wait_recv()

            acc[0:UNIT, :] += mm(cg[kb, rows(u)], turned[kb], NN)

        loop(4, block)
        ug[rows(u), :] = (acc[0:UNIT, :] * act[rows(u), :]).astype(BF)

    def second(u):
        def block(p):
            k = gray(3 - p)
            part[k, rows(u)] = mm(ug[rows(u), :], wu[lane(k)], NN).astype(BF)

            @pl.when(k > 0)
            def _():
                scatter(u, k).start()

        loop(4, block)

    def finish(u):
        total = cg[l, rows(u)].astype(F32) + part[0, rows(u)].astype(F32)
        for k in (1, 3, 2):
            scatter(u, k).wait_recv()
            total += prs[k, rows(u)].astype(F32)
        og[rows(u)] = total.astype(BF)

        @pl.when(odd)
        def _():
            for k in (0, 1, 3, 2):
                cast_down(u, k).start()

        @pl.when(s == 2)
        def _():
            for h in range(2):
                hop(u, h).start()

    def chain(c):
        t, d, h = c // 4, lax.rem(c // 2, 2), lax.rem(c, 2)
        steps = 5 + lax.rem(t + d + 1, 2)
        return t, d, h, steps

    def zcopy(c, k, src):
        d = lax.rem(c // 2, 2)
        return remote(
            src, zrecv.at[c, k], z_s.at[c, k], z_r.at[c, k], {"dp": zdev(2 * d - 1)}
        )

    def local_term(c, k):
        t, d, h, steps = chain(c)
        to = lax.rem(z + (2 * d - 1) * (steps - k) + zn, zn)
        return terms[t, pl.ds(2 * h, 2), to]

    def codes():
        code[0] = mm(ug[...], proj[0], NN).astype(BF)
        for t in range(2):
            def term(kb):
                r = mm(rows_in[t, kb], code[t], TN)
                terms[t, kb] = r.reshape(zn, 64, 128)

            def half_term(h):
                term(2 * h)
                term(2 * h + 1)
                for d in range(2):
                    c = 4 * t + 2 * d + h
                    zsrc[c] = local_term(c, 0).astype(BF)
                    zcopy(c, 0, zsrc.at[c]).start()

            loop(2, half_term)

    last = count - 1

    def unit(u):
        first(u)

        @pl.when((u == last) & (s == 0))
        def _():
            codes()

        second(u)

        @pl.when(u > 0)
        def _():
            finish(u - 1)

    loop(count, unit)

    @pl.when(s > 0)
    def _():
        finish(last)

        @pl.when(s == 2)
        def _():
            pl.semaphore_signal(turn, inc=1, device_id={"segment": 3}, device_id_type=MESH)

        @pl.when(s == 3)
        def _():
            pl.semaphore_wait(turn, 1)

        @pl.when(s > 1)
        def _():
            for k in ORDER:
                gather_in(k).start()
            prep()

        codes()

    def ring_step(i):
        k = i + 1

        def move(c):
            steps = chain(c)[3]

            @pl.when(k < steps)
            def _():
                held = zrecv.at[c, k - 1]
                zcopy(c, k - 1, held).wait_recv()
                zrecv[c, k - 1] = (held[...].astype(F32) + local_term(c, k)).astype(BF)
                zcopy(c, k, held).start()

        loop(8, move)

    loop(5, ring_step)

    def ycopy(t, k):
        return remote(
            ysend.at[t, k], yrecv.at[t, k], y_s.at[t, k], y_r.at[t, k], {"dp": ydev(k)}
        )

    for t in range(2):
        for i in range(4):
            c = 4 * t + i
            zcopy(c, 4 if i // 2 != t else 5, zrecv.at[c, 0]).wait_recv()

        def share(i):
            k = 3 - i
            yo = lax.rem(y + k, 4)
            r = terms[t, yo, z]
            for d in range(2):
                c = (t * 2 + d) * 2 + yo // 2
                r += zrecv[c, 5 if t == d else 4, lax.rem(yo, 2)].astype(F32)

            @pl.when(k > 0)
            def _():
                ysend[t, k] = r.astype(BF)
                ycopy(t, k).start()

            @pl.when(k == 0)
            def _():
                ykeep[t] = r

        loop(4, share)

    pick = lax.broadcasted_iota(jnp.int32, (64, 128), 0) + 64 * lax.rem(z, 2)
    pick = (lax.broadcasted_iota(jnp.int32, (64, 128), 1) == pick).astype(BF)
    at = pl.ds(pl.multiple_of((z // 2) * 128, 128), 128)
    proj2[:, :, 0:128] = proj[...]
    proj2[:, :, 128:256] = proj[...]
    base[0] = mm(pick, wu[y, :, at], NT)
    base[1] = mm(pick, wd[y, :, at], NT)

    @pl.when(s == 0)
    def _():
        finish(last)

    for t in range(2):
        grad = ykeep[t]
        for k in (1, 2, 3):
            ycopy(t, k).wait_recv()
            grad += yrecv[t, k].astype(F32)
        new_first = 0.9 * m1[t] + 0.1 * grad
        new_second = 0.999 * m2[t] + 0.001 * grad * grad
        nfv[t] = new_first
        nsv[t] = new_second
        step = new_first / (jnp.sqrt(new_second) + 1e-08)
        high = step.astype(BF)
        low = (step - high.astype(F32)).astype(BF)
        delta = mm(jnp.concatenate([high, low], axis=1), proj2[t], NT)
        (nup, ndown)[t][...] = (base[t] - 0.05 * delta).astype(BF)

    def drain_unit(u):
        @pl.when(s == 3)
        def _():
            for k in ORDER:
                gather_top(u, k).wait_send()

        @pl.when(s == 1)
        def _():
            for k in ORDER:
                gather_cot(u, k).wait_send()

        @pl.when(odd)
        def _():
            for k in range(4):
                cast_down(u, k).wait_send()

        @pl.when(s == 2)
        def _():
            for h in range(2):
                hop(u, h).wait_send()

        for k in ORDER:
            scatter(u, k).wait_send()

    loop(count, drain_unit)
    for k in ORDER:
        gather_in(k).wait_send()
        for t in range(2):
            ycopy(t, k).wait_send()
    def drain(c):
        def sent(k):
            zcopy(c, k, zsrc.at[c]).wait_send()

        loop(5, sent)

        @pl.when(chain(c)[3] == 6)
        def _():
            sent(5)

    loop(8, drain)


def copy_kernel(*refs):
    half = len(refs) // 2
    sems = refs[-1]
    copies = [
        pltpu.make_async_copy(refs[i], refs[half + i], sems.at[i]) for i in range(half)
    ]
    for c in copies:
        c.start()
    for c in copies:
        c.wait()


def hand_out(*arrays):
    return pl.pallas_call(
        copy_kernel,
        out_shape=tuple(jax.ShapeDtypeStruct(a.shape, a.dtype) for a in arrays),
        in_specs=[pl.BlockSpec(memory_space=pl.ANY)] * len(arrays),
        out_specs=(pl.BlockSpec(memory_space=pl.ANY),) * len(arrays),
        scratch_shapes=[pltpu.SemaphoreType.DMA((len(arrays),))],
        compiler_params=pltpu.CompilerParams(vmem_limit_bytes=2 * 2**20),
        name="hand_out",
    )(*arrays)


def local(zn, inputs, gate_sums, top_grads, up_weight, down_weight, projectors, first_moment, second_moment):
    sds = jax.ShapeDtypeStruct
    any_spec = pl.BlockSpec(memory_space=pl.ANY)
    dma = pltpu.SemaphoreType.DMA
    count = 128 // UNIT
    og, nf, ns, nu, nd = pl.pallas_call(
        functools.partial(kernel, zn),
        out_shape=(
            pltpu.VMEM((128, 768), BF),
            pltpu.VMEM((2, 64, 128), F32),
            pltpu.VMEM((2, 64, 128), F32),
            pltpu.VMEM((64, 816), BF),
            pltpu.VMEM((64, 816), BF),
        ),
        in_specs=[any_spec] * 8,
        out_specs=(pl.BlockSpec(memory_space=pltpu.VMEM),) * 5,
        scratch_shapes=[
            pltpu.VMEM((4, 816, 768), BF),
            pltpu.VMEM((4, 816, 768), BF),
            pltpu.VMEM((2, 816, 128), BF),
            pltpu.VMEM((128, 816), BF),
            pltpu.VMEM((2, 64, 128), F32),
            pltpu.VMEM((2, 64, 128), F32),
            pltpu.VMEM((2, 4, 128, 768), BF),
            pltpu.VMEM((128, 816), F32),
            pltpu.VMEM((128, 816), F32),
            pltpu.VMEM((128, 816), BF),
            pltpu.VMEM((128, 816), BF),
            pltpu.VMEM((4, 128, 768), BF),
            pltpu.VMEM((4, 128, 768), BF),
            pltpu.VMEM((2, 128, 128), BF),
            pltpu.VMEM((2, 4, zn, 64, 128), F32),
            pltpu.VMEM((8, 2, 64, 128), BF),
            pltpu.VMEM((8, 6, 2, 64, 128), BF),
            pltpu.VMEM((2, 4, 64, 128), BF),
            pltpu.VMEM((2, 4, 64, 128), BF),
            pltpu.VMEM((2, 64, 128), F32),
            pltpu.VMEM((2, 64, 816), F32),
            pltpu.VMEM((2, 816, 256), BF),
            pltpu.VMEM((4, 768, 816), BF),
            dma((6,)),
            dma((2, 4)),
            dma((count, 4)),
            dma((count, 4)),
            dma((count, 4)),
            dma((count, 2)),
            dma((count, 2)),
            dma((4,)),
            dma((4,)),
            dma((count, 4)),
            dma((count, 4)),
            dma((8, 6)),
            dma((8, 6)),
            dma((2, 4)),
            dma((2, 4)),
            pltpu.SemaphoreType.REGULAR,
        ],
        compiler_params=pltpu.CompilerParams(
            collective_id=0, has_side_effects=True, vmem_limit_bytes=60 * 2**20
        ),
        name="relay",
    )(
        inputs[0].reshape(128, 768),
        gate_sums[0].reshape(128, 816),
        top_grads.reshape(128, 768),
        jnp.swapaxes(up_weight[0], 0, 1),
        down_weight[0],
        projectors[0],
        jnp.swapaxes(first_moment[0, 0], 1, 2),
        jnp.swapaxes(second_moment[0, 0], 1, 2),
    )
    og, nf, ns, nu, nd = hand_out(og, nf, ns, nu, nd)
    return (
        og.reshape(1, 2, 64, 768),
        jnp.swapaxes(nf, 1, 2)[None, None],
        jnp.swapaxes(ns, 1, 2)[None, None],
        nu[None],
        jnp.swapaxes(nd, 0, 1)[None],
    )


def solution(mesh):
    placed = (
        P("segment", None, "dp", "lane"),
        P("segment", None, "dp", "lane"),
        P(None, "dp", "lane"),
        P("segment", None, "lane"),
        P("segment", "lane", None),
        P("segment", None, "lane", None),
        P("segment", "lane", None, None, "dp"),
        P("segment", "lane", None, None, "dp"),
    )
    return jax.shard_map(
        functools.partial(local, mesh.shape["dp"] // 4),
        mesh=mesh,
        in_specs=placed,
        out_specs=(
            P("segment", None, "dp", "lane"),
            P("segment", "lane", None, None, "dp"),
            P("segment", "lane", None, None, "dp"),
            P("segment", "dp", "lane"),
            P("segment", "lane", "dp"),
        ),
        check_vma=False,
    )
```
